256 devices in a mesh: lat: 8 (over x, y_lo), lon: 32 (over z, y_hi, core).
Axes of the slice: x: 4, y: 4 (y_hi: 2, y_lo: 2; y = y_hi * 2 + y_lo), z: 8, core: 2. Of those that a mesh axis runs over, the one named last changes fastest.
Arguments:
- tokens: bfloat16 [2, 96, 768, 512], P(None, 'lat', 'lon'), may hold values from -6 to 6
- cotangent: bfloat16 [2, 96, 768, 512], P(None, 'lat', 'lon'), may hold values from -6 to 6
- qkv_weights: bfloat16 [2, 512, 1536], replicated, may hold values from -0.25 to 0.25
- proj_weights: bfloat16 [2, 512, 512], replicated, may hold values from -0.25 to 0.25
Outputs:
- d_tokens: bfloat16 [2, 96, 768, 512], P(None, 'lat', 'lon')
- d_qkv: float32 [2, 512, 1536], P(None, 'lat', 'lon')
- d_proj: float32 [2, 512, 512], P(None, 'lat', 'lon')
The draws below stay inside these ranges and needn't reach their ends.
All inputs are finite; a program needn't handle non-finite values.
Results may differ from the reference program's by a relative error of at most 0.03.
Values may be sent and summed in bfloat16 or wider, within the bound.
No kernel may reach another device: no remote copies, remote signals or barrier semaphores. Data moves between devices by JAX's collectives and lax.ppermute only.
A program may use at most 128 MiB of HBM per device.

```python
import jax
import jax.numpy as jnp
from jax import lax

D = 512
HEADS = 8
HEAD_DIM = 64
LEVELS = 2
WIN_LAT = 12
WIN_LON = 6
HALF_LAT = 6
HALF_LON = 3
N_LAT_TOK = 96
N_LON_TOK = 768
N_LAT = 8
N_LON = 32


def spiked(values, own_key, source, target, blocks, factor):
    owner, partner = [(jnp.arange(values.shape[position]) // (values.shape[position] // blocks)).reshape([-1 if axis == position else 1 for axis in range(values.ndim)]) for position in (source, target)]
    chosen = jax.random.permutation(own_key, blocks)[partner]
    strong = (owner == chosen) | (owner == (partner + blocks // 2) % blocks)
    return jnp.where(strong, factor * values, values)


def levels(key, dims, split, smallest, high):
    loudness, own = 1.0, jax.random.fold_in(key, 6)
    for dim, shards_of in split:
        heights = jnp.exp(jax.random.uniform(jax.random.fold_in(own, dim), (shards_of,), jnp.float32, smallest / len(split), high / len(split)))
        loudness = loudness * jnp.repeat(heights, dims[dim] // shards_of).reshape([-1 if axis == dim else 1 for axis in range(len(dims))])
    return loudness


def gaussian(stream_key, shape, scale, reach, pieces=(), kind=jnp.bfloat16):
    drawn = jax.random.normal(stream_key, shape, jnp.float32) * scale
    if len(pieces) > 0:
        drawn = levels(stream_key, shape, pieces, -0.22, 0.18) * drawn
    return jnp.clip(drawn, min=-reach, max=reach).astype(kind)


def bell_draw_with(key, shape, spread, limit, pieces, heavy, held_as=jnp.bfloat16):
    entries = spread * jax.random.normal(key, shape, jnp.float32)
    if pieces:
        entries = entries * levels(key, shape, pieces, -0.22, 0.18)
    return jnp.clip(spiked(entries, jax.random.fold_in(key, 3), *heavy), -limit, limit).astype(held_as)


def setup_inputs(seed: int = 0) -> dict:
    key_of = jax.random.split(jax.random.key(seed), 5)
    tokens = gaussian(key_of[0], (LEVELS, N_LAT_TOK, N_LON_TOK, D), 1.0, 6.0, ((1, 8), (2, 32)))
    cotangent = bell_draw_with(key_of[1], (LEVELS, N_LAT_TOK, N_LON_TOK, D), 1.0, 6.0, ((1, 8), (2, 32)), (2, 3, 32, 2.75))
    qkv_weights = gaussian(key_of[2], (2, D, 3 * D), D ** -0.5, 0.25)
    proj_weights = gaussian(key_of[3], (2, D, D), D ** -0.5, 0.25)
    return dict(tokens=tokens, cotangent=cotangent, qkv_weights=qkv_weights, proj_weights=proj_weights)


EPSILON = 1e-05
MASKED = -1000000000.0

def to_windows(field):
    n_levels, n_rows, n_cols, feature = field.shape
    blocks = field.reshape(n_levels, n_rows // WIN_LAT, WIN_LAT, n_cols // WIN_LON, WIN_LON, feature)
    blocks = blocks.transpose(1, 3, 0, 2, 4, 5)
    return blocks.reshape(n_rows // WIN_LAT * (n_cols // WIN_LON), n_levels * WIN_LAT * WIN_LON, feature)

def from_windows(blocks, n_levels, n_rows, n_cols):
    feature = blocks.shape[-1]
    field = blocks.reshape(n_rows // WIN_LAT, n_cols // WIN_LON, n_levels, WIN_LAT, WIN_LON, feature)
    return field.transpose(2, 0, 3, 1, 4, 5).reshape(n_levels, n_rows, n_cols, feature)

def layer_norm(inputs):
    values_f = inputs.astype(jnp.float32)
    centred = values_f - lax.optimization_barrier(jnp.mean(values_f, axis=-1, keepdims=True))
    inverse = lax.rsqrt(lax.optimization_barrier(jnp.mean(centred * centred, axis=-1, keepdims=True)) + EPSILON)
    return (centred * inverse, inverse)

def split_heads(part):
    return part.reshape(part.shape[0], part.shape[1], HEADS, -1).astype(jnp.float32)

def attend(normed, w_qkv, labels):
    packed = jnp.dot(normed, w_qkv, preferred_element_type=jnp.float32).astype(jnp.bfloat16)
    queries = split_heads(packed[..., :D])
    keys_h = split_heads(packed[..., D:2 * D])
    values_h = split_heads(packed[..., 2 * D:])
    score_scale = HEAD_DIM ** (-0.5)
    scores = jnp.einsum('wqhd,wkhd->whqk', queries, keys_h) * score_scale
    same_group = labels[:, None, :, None] == labels[:, None, None, :]
    scores = jnp.where(same_group, scores, MASKED)
    soft_probs = jax.nn.softmax(scores, axis=-1)
    probs_low = soft_probs.astype(jnp.bfloat16)
    mixed_out = jnp.einsum('whqk,wkhd->wqhd', probs_low.astype(jnp.float32), values_h).astype(jnp.bfloat16)
    mixed_out = mixed_out.reshape(mixed_out.shape[0], mixed_out.shape[1], -1)
    return ((queries, keys_h, values_h), soft_probs, probs_low, mixed_out)

def block_forward(inputs, labels, w_qkv, w_proj):
    standard = layer_norm(inputs)[0]
    normed = standard.astype(jnp.bfloat16)
    mixed_out = attend(normed, w_qkv, labels)[3]
    return (inputs.astype(jnp.float32) + jnp.dot(mixed_out, w_proj, preferred_element_type=jnp.float32)).astype(jnp.bfloat16)

def block_backward(inputs, upstream, labels, w_qkv, w_proj):
    standard, inverse = layer_norm(inputs)
    normed = standard.astype(jnp.bfloat16)
    heads, soft_probs, probs_low, mixed_out = attend(normed, w_qkv, labels)
    queries, keys_h, values_h = heads
    feature = inputs.shape[-1]
    grad_proj = jnp.dot(mixed_out.reshape(-1, feature).T, upstream.reshape(-1, feature), preferred_element_type=jnp.float32)
    d_mixed = jnp.dot(upstream, w_proj.T, preferred_element_type=jnp.float32).astype(jnp.bfloat16)
    d_heads = split_heads(d_mixed)
    d_probs = jnp.einsum('wqhd,wkhd->whqk', d_heads, values_h)
    d_values = jnp.einsum('whqk,wqhd->wkhd', probs_low.astype(jnp.float32), d_heads)
    score_scale = HEAD_DIM ** (-0.5)
    d_scores = (soft_probs * (d_probs - lax.optimization_barrier(jnp.sum(soft_probs * d_probs, axis=-1, keepdims=True))) * score_scale).astype(jnp.bfloat16)
    d_scores = d_scores.astype(jnp.float32)
    d_queries = jnp.einsum('whqk,wkhd->wqhd', d_scores, keys_h)
    d_keys = jnp.einsum('whqk,wqhd->wkhd', d_scores, queries)
    n_win, n_tok = (inputs.shape[0], inputs.shape[1])
    d_packed = jnp.concatenate([d_queries.reshape(n_win, n_tok, -1), d_keys.reshape(n_win, n_tok, -1), d_values.reshape(n_win, n_tok, -1)], axis=-1).astype(jnp.bfloat16)
    grad_qkv = jnp.dot(normed.reshape(-1, feature).T, d_packed.reshape(-1, 3 * feature), preferred_element_type=jnp.float32)
    d_normed = jnp.dot(d_packed, w_qkv.T, preferred_element_type=jnp.float32)
    d_input = inverse * (d_normed - lax.optimization_barrier(jnp.mean(d_normed, axis=-1, keepdims=True)) - standard * lax.optimization_barrier(jnp.mean(d_normed * standard, axis=-1, keepdims=True)))
    result = (upstream.astype(jnp.float32) + d_input).astype(jnp.bfloat16)
    return (result, grad_qkv, grad_proj)

def grouped(array_in):
    groups = N_LAT * N_LON
    return array_in.reshape((groups, -1) + array_in.shape[1:])

def forward_groups(inputs, labels, w_qkv, w_proj):

    def single(group):
        return block_forward(group[0], group[1], w_qkv, w_proj)
    results = lax.map(single, (grouped(inputs), grouped(labels)))
    return results.reshape(inputs.shape)

def backward_groups(inputs, upstream, labels, w_qkv, w_proj):

    def step(carry, group):
        result, grad_qkv, grad_proj = block_backward(group[0], group[1], group[2], w_qkv, w_proj)
        return ((carry[0] + grad_qkv, carry[1] + grad_proj), result)
    start = (jnp.zeros((D, 3 * D), jnp.float32), jnp.zeros((D, D), jnp.float32))
    totals, results = lax.scan(step, start, (grouped(inputs), grouped(upstream), grouped(labels)))
    return (results.reshape(inputs.shape), totals[0], totals[1])

def reference(tokens, cotangent, qkv_weights, proj_weights):
    n_levels, n_rows, n_cols, feature = tokens.shape
    plain_tokens = to_windows(tokens)
    plain_labels = jnp.zeros(plain_tokens.shape[:2], jnp.int32)
    first_out = from_windows(forward_groups(plain_tokens, plain_labels, qkv_weights[0], proj_weights[0]), n_levels, n_rows, n_cols)
    rolled_first = jnp.roll(first_out, (-HALF_LAT, -HALF_LON), axis=(1, 2))
    rolled_cot = jnp.roll(cotangent, (-HALF_LAT, -HALF_LON), axis=(1, 2))
    row_index = lax.broadcasted_iota(jnp.int32, (n_levels, n_rows, n_cols, 1), 1)
    wrapped = jnp.where(row_index >= n_rows - HALF_LAT, 1, 0).astype(jnp.int32)
    shifted_labels = to_windows(wrapped)[..., 0]
    d_moved, grad_qkv_two, grad_proj_two = backward_groups(to_windows(rolled_first), to_windows(rolled_cot), shifted_labels, qkv_weights[1], proj_weights[1])
    d_first = jnp.roll(from_windows(d_moved, n_levels, n_rows, n_cols), (HALF_LAT, HALF_LON), axis=(1, 2))
    d_plain, grad_qkv_one, grad_proj_one = backward_groups(plain_tokens, to_windows(d_first), plain_labels, qkv_weights[0], proj_weights[0])
    d_tokens = from_windows(d_plain, n_levels, n_rows, n_cols)
    return (d_tokens, jnp.stack([grad_qkv_one, grad_qkv_two]), jnp.stack([grad_proj_one, grad_proj_two]))
```

```python
import functools

import jax
import jax.numpy as jnp
import numpy as np
from jax import lax
from jax.experimental import pallas as pl
from jax.experimental.pallas import tpu as pltpu
from jax.sharding import PartitionSpec as P

D = 512
HEADS = 8
HEAD_DIM = 64
LEVELS = 2
WIN_LAT = 12
WIN_LON = 6
HALF_LAT = 6
HALF_LON = 3
ROWS = 12
COLS = 24
TOKENS = LEVELS * ROWS * COLS
WINDOW = LEVELS * WIN_LAT * WIN_LON
WINDOWS = TOKENS // WINDOW
HALF = TOKENS // 2
STRIP = LEVELS * HALF_LAT * HALF_LON
SOURCE = 2 * HALF + 2 * STRIP
QUAD = 4 * HEAD_DIM
EPSILON = 1e-05
MASKED = -1000000000.0
SCALE = HEAD_DIM ** (-0.5)
F32 = jnp.float32
BF16 = jnp.bfloat16


def window_order(level, row, col):
    return (col // WIN_LON) * WINDOW + (level * WIN_LAT + row) * WIN_LON + col % WIN_LON


def plain_matrix():
    out = np.zeros((TOKENS, TOKENS), np.float32)
    for level, row, col in np.ndindex(LEVELS, ROWS, COLS):
        out[window_order(level, row, col), (level * ROWS + row) * COLS + col] = 1
    return out


def piece_index(level, row, col, narrow):
    upper = row < HALF_LAT
    at = level * HALF_LAT + row % HALF_LAT
    if narrow:
        return 2 * HALF + (STRIP if upper else 0) + at * HALF_LON + col
    return (HALF if upper else 0) + at * COLS + col


def cut_matrix():
    out = np.zeros((SOURCE, TOKENS), np.float32)
    for level, row, col in np.ndindex(LEVELS, ROWS, COLS):
        out[piece_index(level, row, col, False), window_order(level, row, col)] = 1
        if col < HALF_LON:
            out[piece_index(level, row, col, True), window_order(level, row, col)] = 1
    return out


def shifted_matrix():
    out = np.zeros((TOKENS, SOURCE), np.float32)
    for level, row, col in np.ndindex(LEVELS, ROWS, COLS):
        from_row, from_col = (row + HALF_LAT) % ROWS, col + HALF_LON
        place = piece_index(level, from_row, from_col % COLS, from_col >= COLS)
        out[window_order(level, row, col), place] = 1
    return out


def joined_matrix():
    out = np.zeros((TOKENS, SOURCE), np.float32)
    for level, row, col in np.ndindex(LEVELS, ROWS, COLS):
        out[window_order(level, row, col), piece_index(level, row, col, col < HALF_LON)] = 1
    return out


def dot(a, b):
    return lax.dot_general(a, b, (((1,), (0,)), ((), ())), preferred_element_type=F32)


def dot_nt(a, b):
    return lax.dot_general(a, b, (((1,), (1,)), ((), ())), preferred_element_type=F32)


def dot_tn(a, b):
    return lax.dot_general(a, b, (((0,), (0,)), ((), ())), preferred_element_type=F32)


def layer_norm(values):
    centred = values - jnp.mean(values, axis=-1, keepdims=True)
    inverse = lax.rsqrt(jnp.mean(centred * centred, axis=-1, keepdims=True) + EPSILON)
    return centred * inverse, inverse


def head_of_lane(rows):
    return lax.broadcasted_iota(jnp.int32, (rows, QUAD), 1) // HEAD_DIM


def stacked(part, scale):
    lane = head_of_lane(1)
    wide = [part * jnp.where(lane == h, scale, 0.0).astype(BF16) for h in range(4)]
    return jnp.concatenate(wide, axis=0)


def unstacked(product):
    lane = head_of_lane(WINDOW)
    out = product[:WINDOW]
    for h in range(1, 4):
        out = jnp.where(lane == h, product[h * WINDOW : (h + 1) * WINDOW], out)
    return out


def soft(keys_stacked, queries, bias):
    scores = dot_nt(keys_stacked, queries).reshape(4, WINDOW, WINDOW)
    if bias is not None:
        scores = scores + bias[None]
    top = jnp.max(scores, axis=1, keepdims=True)
    raised = jnp.exp(scores - top)
    return raised * (1.0 / jnp.sum(raised, axis=1, keepdims=True))


def forward_kernel(tokens, w_qkv, w_proj, plain, cut, pieces, packed_out):
    values = dot(plain[...], tokens[...])
    normed = layer_norm(values)[0].astype(BF16)
    packed = dot(normed, w_qkv[...]).astype(BF16)
    packed_out[...] = packed
    rows = []
    for w in range(WINDOWS):
        cols = []
        for quad in range(2):
            part = [
                packed_out[w * WINDOW : (w + 1) * WINDOW, n * D + quad * QUAD : n * D + (quad + 1) * QUAD]
                for n in range(3)
            ]
            probs = soft(stacked(part[1], SCALE), part[0], None).astype(BF16)
            cols.append(dot_tn(probs.reshape(4 * WINDOW, WINDOW), stacked(part[2], 1.0)).astype(BF16))
        rows.append(jnp.concatenate(cols, axis=1))
    mixed = jnp.concatenate(rows, axis=0)
    first = (values + dot(mixed, w_proj[...])).astype(BF16)
    pieces[...] = dot(cut[...], first).astype(BF16)


def backward_kernel(*refs, masked, saved):
    refs = list(refs)
    inputs, upstream, w_qkv, w_proj, gather_u, gather_g, scatter = refs[:7]
    refs = refs[7:]
    bias = refs.pop(0)[...] if masked else None
    packed_in = refs.pop(0) if saved else None
    d_out, grad_qkv, grad_proj, mixed_ref, d_mixed_ref, d_packed_ref = refs[:6]
    values = dot(gather_u[...], inputs[...])
    standard, inverse = layer_norm(values)
    normed = standard.astype(BF16)
    if saved:
        packed_ref = packed_in
    else:
        packed_ref = refs[6]
        packed_ref[...] = dot(normed, w_qkv[...]).astype(BF16)
    gradient = dot(gather_g[...], upstream[...])
    low = gradient.astype(BF16)
    d_mixed_ref[...] = dot_nt(low, w_proj[...]).astype(BF16)
    for w in range(WINDOWS):
        span = slice(w * WINDOW, (w + 1) * WINDOW)
        for quad in range(2):
            at = [slice(n * D + quad * QUAD, n * D + (quad + 1) * QUAD) for n in range(3)]
            queries, keys, vals = [packed_ref[span, at[n]] for n in range(3)]
            d_mixed = d_mixed_ref[span, at[0]]
            keys_stacked, vals_stacked = stacked(keys, SCALE), stacked(vals, 1.0)
            probs = soft(keys_stacked, queries, bias)
            probs_low = probs.astype(BF16).reshape(4 * WINDOW, WINDOW)
            mixed_ref[span, at[0]] = dot_tn(probs_low, vals_stacked).astype(BF16)
            d_probs = dot_nt(vals_stacked, d_mixed).reshape(4, WINDOW, WINDOW)
            inner = jnp.sum(probs * d_probs, axis=1, keepdims=True)
            d_scores = (probs * (d_probs - inner)).astype(BF16).reshape(4 * WINDOW, WINDOW)
            d_packed_ref[span, at[0]] = dot_tn(d_scores, keys_stacked).astype(BF16)
            d_packed_ref[span, at[1]] = (unstacked(dot(d_scores, queries)) * SCALE).astype(BF16)
            d_packed_ref[span, at[2]] = unstacked(dot(probs_low, d_mixed)).astype(BF16)
    d_packed = d_packed_ref[...]
    grad_proj[...] = dot_tn(mixed_ref[...], low).astype(BF16)
    grad_qkv[...] = dot_tn(normed, d_packed).astype(BF16)
    d_normed = dot_nt(d_packed, w_qkv[...])
    d_input = inverse * (
        d_normed
        - jnp.mean(d_normed, axis=-1, keepdims=True)
        - standard * jnp.mean(d_normed * standard, axis=-1, keepdims=True)
    )
    d_out[...] = dot_tn(scatter[...], (gradient + d_input).astype(BF16)).astype(BF16)


def shape(*dims, kind=BF16):
    return jax.ShapeDtypeStruct(dims, kind)


PARAMS = pltpu.CompilerParams(vmem_limit_bytes=48 * 1024 * 1024)


def forward(tokens, w_qkv, w_proj, plain, cut):
    return pl.pallas_call(
        forward_kernel,
        out_shape=(shape(SOURCE, D), shape(TOKENS, 3 * D)),
        compiler_params=PARAMS,
        name="forward",
    )(tokens, w_qkv, w_proj, plain, cut)


def backward(inputs, upstream, w_qkv, w_proj, gather_u, gather_g, scatter, bias=None, packed=None):
    extra = [x for x in (bias, packed) if x is not None]
    scratch = [pltpu.VMEM((TOKENS, D), BF16), pltpu.VMEM((TOKENS, D), BF16), pltpu.VMEM((TOKENS, 3 * D), BF16)]
    if packed is None:
        scratch.append(pltpu.VMEM((TOKENS, 3 * D), BF16))
    return pl.pallas_call(
        functools.partial(backward_kernel, masked=bias is not None, saved=packed is not None),
        out_shape=(shape(scatter.shape[1], D), shape(D, 3 * D), shape(D, D)),
        scratch_shapes=scratch,
        compiler_params=PARAMS,
        name="backward_shifted" if packed is None else "backward_plain",
    )(inputs, upstream, w_qkv, w_proj, gather_u, gather_g, scatter, *extra)


def moved(piece, lat, lon):
    axes, n_lat, n_lon = ("lat", "lon"), lax.axis_size("lat"), lax.axis_size("lon")
    route = [
        (a * n_lon + b, (a + lat) % n_lat * n_lon + (b + lon) % n_lon)
        for a in range(n_lat)
        for b in range(n_lon)
    ]
    return lax.ppermute(piece, axes, route)


def exchanged(pieces, step):
    tall = moved(pieces[1], step, 0)
    side = moved(pieces[2], 0, step)
    corner = moved(pieces[3], step, step)
    return jnp.concatenate([pieces[0], tall, side, corner], axis=0)


def cut_pieces(joint):
    return [joint[:HALF], joint[HALF : 2 * HALF], joint[2 * HALF : 2 * HALF + STRIP], joint[2 * HALF + STRIP :]]


def field_pieces(field):
    low, up = field[:, HALF_LAT:], field[:, :HALF_LAT]
    parts = [low, up, low[:, :, :HALF_LON], up[:, :, :HALF_LON]]
    return [part.reshape(-1, D) for part in parts]


def reduce_grads(grad_qkv, grad_proj):
    parts = [lax.psum_scatter(x, "lat", scatter_dimension=0, tiled=True) for x in (grad_qkv, grad_proj)]
    return [lax.psum_scatter(x, "lon", scatter_dimension=1, tiled=True).astype(F32) for x in parts]


def body(tokens, cotangent, qkv_weights, proj_weights):
    plain, cut, shift, join = [
        jnp.asarray(make(), BF16) for make in (plain_matrix, cut_matrix, shifted_matrix, joined_matrix)
    ]
    upstream = exchanged(field_pieces(cotangent), -1)
    flat = tokens.reshape(TOKENS, D)
    pieces, packed = forward(flat, qkv_weights[0], proj_weights[0], plain, cut)
    first = exchanged(cut_pieces(pieces), -1)
    last_lat = lax.axis_index("lat") == lax.axis_size("lat") - 1
    label = (np.arange(WINDOW) // WIN_LON % WIN_LAT >= HALF_LAT).astype(np.int32)
    bias = jnp.where(last_lat & (label[:, None] != label[None, :]), MASKED, 0.0).astype(F32)
    d_moved, grad_qkv_two, grad_proj_two = backward(
        first, upstream, qkv_weights[1], proj_weights[1], shift, shift, shift, bias=bias
    )
    reduced_two = reduce_grads(grad_qkv_two, grad_proj_two)
    d_first = exchanged(cut_pieces(d_moved), 1)
    d_tokens, grad_qkv_one, grad_proj_one = backward(
        flat, d_first, qkv_weights[0], proj_weights[0], plain, join, plain, packed=packed
    )
    reduced_one = reduce_grads(grad_qkv_one, grad_proj_one)
    return (
        d_tokens.reshape(tokens.shape),
        jnp.stack([reduced_one[0], reduced_two[0]]),
        jnp.stack([reduced_one[1], reduced_two[1]]),
    )


def solution(mesh):
    return jax.shard_map(
        body,
        mesh=mesh,
        in_specs=(P(None, "lat", "lon", None), P(None, "lat", "lon", None), P(), P()),
        out_specs=(P(None, "lat", "lon", None), P(None, "lat", "lon"), P(None, "lat", "lon")),
        check_vma=False,
    )
```

```python
import functools

import jax
import jax.numpy as jnp
import numpy as np
from jax import lax
from jax.experimental import pallas as pl
from jax.experimental.pallas import tpu as pltpu
from jax.sharding import PartitionSpec as P

D = 512
HEADS = 8
HEAD_DIM = 64
LEVELS = 2
WIN_LAT = 12
WIN_LON = 6
HALF_LAT = 6
HALF_LON = 3
ROWS = 12
COLS = 24
TOKENS = LEVELS * ROWS * COLS
WINDOW = LEVELS * WIN_LAT * WIN_LON
WINDOWS = TOKENS // WINDOW
HALF = TOKENS // 2
STRIP = LEVELS * HALF_LAT * HALF_LON
SOURCE = 2 * HALF + 2 * STRIP
QUAD = 4 * HEAD_DIM
EPSILON = 1e-05
MASKED = -1000000000.0
SCALE = HEAD_DIM ** (-0.5)
F32 = jnp.float32
BF16 = jnp.bfloat16


def window_order(level, row, col):
    return (col // WIN_LON) * WINDOW + (level * WIN_LAT + row) * WIN_LON + col % WIN_LON


def plain_matrix():
    out = np.zeros((TOKENS, TOKENS), np.float32)
    for level, row, col in np.ndindex(LEVELS, ROWS, COLS):
        out[window_order(level, row, col), (level * ROWS + row) * COLS + col] = 1
    return out


def piece_index(level, row, col, narrow):
    upper = row < HALF_LAT
    at = level * HALF_LAT + row % HALF_LAT
    if narrow:
        return 2 * HALF + (STRIP if upper else 0) + at * HALF_LON + col
    return (HALF if upper else 0) + at * COLS + col


def cut_matrix():
    out = np.zeros((SOURCE, TOKENS), np.float32)
    for level, row, col in np.ndindex(LEVELS, ROWS, COLS):
        out[piece_index(level, row, col, False), window_order(level, row, col)] = 1
        if col < HALF_LON:
            out[piece_index(level, row, col, True), window_order(level, row, col)] = 1
    return out


def shifted_matrix():
    out = np.zeros((TOKENS, SOURCE), np.float32)
    for level, row, col in np.ndindex(LEVELS, ROWS, COLS):
        from_row, from_col = (row + HALF_LAT) % ROWS, col + HALF_LON
        place = piece_index(level, from_row, from_col % COLS, from_col >= COLS)
        out[window_order(level, row, col), place] = 1
    return out


def joined_matrix():
    out = np.zeros((TOKENS, SOURCE), np.float32)
    for level, row, col in np.ndindex(LEVELS, ROWS, COLS):
        out[window_order(level, row, col), piece_index(level, row, col, col < HALF_LON)] = 1
    return out


def dot(a, b):
    return lax.dot_general(a, b, (((1,), (0,)), ((), ())), preferred_element_type=F32)


def dot_nt(a, b):
    return lax.dot_general(a, b, (((1,), (1,)), ((), ())), preferred_element_type=F32)


def dot_tn(a, b):
    return lax.dot_general(a, b, (((0,), (0,)), ((), ())), preferred_element_type=F32)


def layer_norm(values):
    centred = values - jnp.mean(values, axis=-1, keepdims=True)
    inverse = lax.rsqrt(jnp.mean(centred * centred, axis=-1, keepdims=True) + EPSILON)
    return centred * inverse, inverse


def head_of_lane(rows):
    return lax.broadcasted_iota(jnp.int32, (rows, QUAD), 1) // HEAD_DIM


def stacked(part, scale):
    lane = head_of_lane(1)
    wide = [part * jnp.where(lane == h, scale, 0.0).astype(BF16) for h in range(4)]
    return jnp.concatenate(wide, axis=0)


def unstacked(product):
    lane = head_of_lane(WINDOW)
    out = product[:WINDOW]
    for h in range(1, 4):
        out = jnp.where(lane == h, product[h * WINDOW : (h + 1) * WINDOW], out)
    return out


def soft(keys_stacked, queries, bias):
    scores = dot_nt(keys_stacked, queries).reshape(4, WINDOW, WINDOW)
    if bias is not None:
        scores = scores + bias[None]
    top = jnp.max(scores, axis=1, keepdims=True)
    raised = jnp.exp(scores - top)
    return raised * (1.0 / jnp.sum(raised, axis=1, keepdims=True))


def forward_kernel(tokens, w_qkv, w_proj, plain, cut, pieces, packed_out):
    values = dot(plain[...], tokens[...])
    normed = layer_norm(values)[0].astype(BF16)
    packed = dot(normed, w_qkv[...]).astype(BF16)
    packed_out[...] = packed
    rows = []
    for w in range(WINDOWS):
        cols = []
        for quad in range(2):
            part = [
                packed_out[w * WINDOW : (w + 1) * WINDOW, n * D + quad * QUAD : n * D + (quad + 1) * QUAD]
                for n in range(3)
            ]
            probs = soft(stacked(part[1], SCALE), part[0], None).astype(BF16)
            cols.append(dot_tn(probs.reshape(4 * WINDOW, WINDOW), stacked(part[2], 1.0)).astype(BF16))
        rows.append(jnp.concatenate(cols, axis=1))
    mixed = jnp.concatenate(rows, axis=0)
    first = (values + dot(mixed, w_proj[...])).astype(BF16)
    pieces[...] = dot(cut[...], first).astype(BF16)


def backward_kernel(*refs, masked, saved):
    refs = list(refs)
    core, inputs, upstream, w_qkv, w_proj, gather_u, gather_g, scatter = refs[:8]
    refs = refs[8:]
    bias = refs.pop(0)[...] if masked else None
    packed_in = refs.pop(0) if saved else None
    d_out, kept, sent, mixed_ref, d_mixed_ref, d_packed_ref, grads = refs[:7]
    values = dot(gather_u[...], inputs[...])
    standard, inverse = layer_norm(values)
    normed = standard.astype(BF16)
    if saved:
        packed_ref = packed_in
    else:
        packed_ref = refs[7]
        packed_ref[...] = dot(normed, w_qkv[...]).astype(BF16)
    gradient = dot(gather_g[...], upstream[...])
    low = gradient.astype(BF16)
    d_mixed_ref[...] = dot_nt(low, w_proj[...]).astype(BF16)
    for w in range(WINDOWS):
        span = slice(w * WINDOW, (w + 1) * WINDOW)
        for quad in range(2):
            at = [slice(n * D + quad * QUAD, n * D + (quad + 1) * QUAD) for n in range(3)]
            queries, keys, vals = [packed_ref[span, at[n]] for n in range(3)]
            d_mixed = d_mixed_ref[span, at[0]]
            keys_stacked, vals_stacked = stacked(keys, SCALE), stacked(vals, 1.0)
            probs = soft(keys_stacked, queries, bias)
            probs_low = probs.astype(BF16).reshape(4 * WINDOW, WINDOW)
            mixed_ref[span, at[0]] = dot_tn(probs_low, vals_stacked).astype(BF16)
            d_probs = dot_nt(vals_stacked, d_mixed).reshape(4, WINDOW, WINDOW)
            inner = jnp.sum(probs * d_probs, axis=1, keepdims=True)
            d_scores = (probs * (d_probs - inner)).astype(BF16).reshape(4 * WINDOW, WINDOW)
            d_packed_ref[span, at[0]] = dot_tn(d_scores, keys_stacked).astype(BF16)
            d_packed_ref[span, at[1]] = (unstacked(dot(d_scores, queries)) * SCALE).astype(BF16)
            d_packed_ref[span, at[2]] = unstacked(dot(probs_low, d_mixed)).astype(BF16)
    d_packed = d_packed_ref[...]
    grads[:, :48] = dot_tn(d_packed, normed).astype(BF16).reshape(32, 48, D)
    grads[:, 48:] = dot_tn(low, mixed_ref[...]).astype(BF16).reshape(32, 16, D)
    for j in range(16):
        kept[j] = grads[2 * j + core[0]]
        sent[j] = grads[2 * j + 1 - core[0]]
    d_normed = dot_nt(d_packed, w_qkv[...])
    d_input = inverse * (
        d_normed
        - jnp.mean(d_normed, axis=-1, keepdims=True)
        - standard * jnp.mean(d_normed * standard, axis=-1, keepdims=True)
    )
    d_out[...] = dot_tn(scatter[...], (gradient + d_input).astype(BF16)).astype(BF16)


def shape(*dims, kind=BF16):
    return jax.ShapeDtypeStruct(dims, kind)


PARAMS = pltpu.CompilerParams(vmem_limit_bytes=48 * 1024 * 1024)


def forward(tokens, w_qkv, w_proj, plain, cut):
    return pl.pallas_call(
        forward_kernel,
        out_shape=(shape(SOURCE, D), shape(TOKENS, 3 * D)),
        compiler_params=PARAMS,
        name="forward",
    )(tokens, w_qkv, w_proj, plain, cut)


def backward(inputs, upstream, w_qkv, w_proj, gather_u, gather_g, scatter, bias=None, packed=None):
    extra = [x for x in (bias, packed) if x is not None]
    scratch = [pltpu.VMEM((TOKENS, width), BF16) for width in (D, D, 3 * D)] + [pltpu.VMEM((32, 64, D), BF16)]
    core = (lax.axis_index("lon") % 2).astype(jnp.int32).reshape(1)
    if packed is None:
        scratch.append(pltpu.VMEM((TOKENS, 3 * D), BF16))
    d_out, kept, sent = pl.pallas_call(
        functools.partial(backward_kernel, masked=bias is not None, saved=packed is not None),
        out_shape=(shape(scatter.shape[1], D), shape(16, 64, D), shape(16, 64, D)),
        in_specs=[pl.BlockSpec(memory_space=pltpu.SMEM)]
        + [pl.BlockSpec(memory_space=pltpu.VMEM)] * (7 + len(extra)),
        scratch_shapes=scratch,
        compiler_params=PARAMS,
        name="backward_shifted" if packed is None else "backward_plain",
    )(core, inputs, upstream, w_qkv, w_proj, gather_u, gather_g, scatter, *extra)
    return d_out, kept.reshape(1024, D), sent.reshape(1024, D)


def moved(piece, lat, lon):
    axes, n_lat, n_lon = ("lat", "lon"), lax.axis_size("lat"), lax.axis_size("lon")
    route = [
        (a * n_lon + b, (a + lat) % n_lat * n_lon + (b + lon) % n_lon)
        for a in range(n_lat)
        for b in range(n_lon)
    ]
    return lax.ppermute(piece, axes, route)


def exchanged(pieces, step):
    tall = moved(pieces[1], step, 0)
    side = moved(pieces[2], 0, step)
    corner = moved(pieces[3], step, step)
    return jnp.concatenate([pieces[0], tall, side, corner], axis=0)


def cut_pieces(joint):
    return [joint[:HALF], joint[HALF : 2 * HALF], joint[2 * HALF : 2 * HALF + STRIP], joint[2 * HALF + STRIP :]]


def field_pieces(field):
    low, up = field[:, HALF_LAT:], field[:, :HALF_LAT]
    parts = [low, up, low[:, :, :HALF_LON], up[:, :, :HALF_LON]]
    return [part.reshape(-1, D) for part in parts]


def swapped_halves(top, bottom):
    left = lax.broadcasted_iota(jnp.int32, top.shape, 1) < top.shape[1] // 2
    turned = [pltpu.roll(x, top.shape[1] // 2, 1) for x in (top, bottom)]
    return jnp.where(left, top, turned[1]), jnp.where(left, turned[0], bottom)


def core_sum_kernel(place, kept, received, *refs):
    outs, held = refs[:-1], refs[-1]
    half = kept.shape[0] // 2
    for pair in range(4):
        at = slice(pair * 128, (pair + 1) * 128)
        total = kept[:, at].astype(F32) + received[:, at].astype(F32)
        even, odd = swapped_halves(total[:half], total[half:])
        held[2 * pair] = even.astype(BF16)
        held[2 * pair + 1] = odd.astype(BF16)
    for step in range(8):
        outs[step][...] = held[jnp.bitwise_xor(place[0], step)]


def lat_sum_kernel(*refs):
    parts, out = refs[:-1], refs[-1]
    total = parts[0][...].astype(F32)
    for part in parts[1:]:
        total = total + part[...].astype(F32)
    for j in range(8):
        one, other = swapped_halves(total[64 * j : 64 * j + 32], total[64 * j + 32 : 64 * j + 64])
        out[j] = one.astype(BF16)
        out[j + 8] = other.astype(BF16)


def lon_sum_kernel(parts, grad_qkv, grad_proj):
    for block in range(2):
        total = parts[0, block].astype(F32)
        for j in range(1, 16):
            total = total + parts[j, block].astype(F32)
        whole = jnp.concatenate([total, pltpu.roll(total, 64, 1)], axis=0)
        across = whole.T[:64]
        grad_qkv[block] = across[:, :48]
        grad_proj[block] = across[:, 48:]


def core_reduced(kept, sent):
    place = lax.axis_index("lat").astype(jnp.int32).reshape(1)
    received = lax.ppermute(sent, "lon", [(i, i ^ 1) for i in range(lax.axis_size("lon"))])
    piece = shape(512, 128)
    return pl.pallas_call(
        core_sum_kernel,
        out_shape=(piece,) * 8,
        in_specs=[pl.BlockSpec(memory_space=pltpu.SMEM)] + [pl.BlockSpec(memory_space=pltpu.VMEM)] * 2,
        scratch_shapes=[pltpu.VMEM((8, 512, 128), BF16)],
        compiler_params=PARAMS,
        name="core_sum",
    )(place, kept, received)


def lat_reduced(chunks):
    arrived = [chunks[0]]
    for step in (7, 6, 5, 4, 3, 2, 1):
        arrived.append(lax.ppermute(chunks[step], "lat", [(i, i ^ step) for i in range(lax.axis_size("lat"))]))
    return pl.pallas_call(
        lat_sum_kernel, out_shape=shape(16, 32, 128), compiler_params=PARAMS, name="lat_sum"
    )(*arrived)


def lon_reduced(one, two):
    both = jnp.stack([one, two], axis=1)
    groups = [[2 * j + core for j in range(16)] for core in range(2)]
    arrived = lax.all_to_all(both, "lon", 0, 0, tiled=True, axis_index_groups=groups)
    return pl.pallas_call(
        lon_sum_kernel,
        out_shape=(shape(2, 64, 48, kind=F32), shape(2, 64, 16, kind=F32)),
        compiler_params=PARAMS,
        name="lon_sum",
    )(arrived)


def body(tokens, cotangent, qkv_weights, proj_weights):
    plain, cut, shift, join = [
        jnp.asarray(make(), BF16) for make in (plain_matrix, cut_matrix, shifted_matrix, joined_matrix)
    ]
    upstream = exchanged(field_pieces(cotangent), -1)
    flat = tokens.reshape(TOKENS, D)
    pieces, packed = forward(flat, qkv_weights[0], proj_weights[0], plain, cut)
    first = exchanged(cut_pieces(pieces), -1)
    last_lat = lax.axis_index("lat") == lax.axis_size("lat") - 1
    label = (np.arange(WINDOW) // WIN_LON % WIN_LAT >= HALF_LAT).astype(np.int32)
    bias = jnp.where(last_lat & (label[:, None] != label[None, :]), MASKED, 0.0).astype(F32)
    d_moved, kept_two, sent_two = backward(
        first, upstream, qkv_weights[1], proj_weights[1], shift, shift, shift, bias=bias
    )
    d_first = exchanged(cut_pieces(d_moved), 1)
    chunks_two = core_reduced(kept_two, sent_two)
    d_first, chunks_two = lax.optimization_barrier((d_first, chunks_two))
    reduced_two = lat_reduced(chunks_two)
    d_tokens, kept_one, sent_one = backward(
        flat, d_first, qkv_weights[0], proj_weights[0], plain, join, plain, packed=packed
    )
    reduced_one = lat_reduced(core_reduced(kept_one, sent_one))
    grad_qkv, grad_proj = lon_reduced(reduced_one, reduced_two)
    return d_tokens.reshape(tokens.shape), grad_qkv, grad_proj


def solution(mesh):
    return jax.shard_map(
        body,
        mesh=mesh,
        in_specs=(P(None, "lat", "lon", None), P(None, "lat", "lon", None), P(), P()),
        out_specs=(P(None, "lat", "lon", None), P(None, "lat", "lon"), P(None, "lat", "lon")),
        check_vma=False,
    )
```

```python
import functools

import jax
import jax.numpy as jnp
import numpy as np
from jax import lax
from jax.experimental import pallas as pl
from jax.experimental.pallas import tpu as pltpu
from jax.sharding import PartitionSpec as P

D = 512
HEADS = 8
HEAD_DIM = 64
LEVELS = 2
WIN_LAT = 12
WIN_LON = 6
HALF_LAT = 6
HALF_LON = 3
ROWS = 12
COLS = 24
TOKENS = LEVELS * ROWS * COLS
WINDOW = LEVELS * WIN_LAT * WIN_LON
WINDOWS = TOKENS // WINDOW
HALF = TOKENS // 2
QUAD = 4 * HEAD_DIM
LEVEL = ROWS * COLS
SEGMENT = WIN_LAT * WIN_LON
WIDE = 128
STRIP = 32
PIECES = 2 * WIDE + 2 * STRIP
EPSILON = 1e-05
MASKED = -1000000000.0
SCALE = HEAD_DIM ** (-0.5)
LARGE = 58
SMALL = 6
PEAK_FLOPS = 1_150_000_000
PEAK_BYTES = 3_690_000
F32 = jnp.float32
BF16 = jnp.bfloat16


def window_order(row, col):
    return (col // WIN_LON) * SEGMENT + row * WIN_LON + col % WIN_LON


def field_order(row, col):
    return row * COLS + col


def piece_order(row, col):
    upper = int(row < HALF_LAT)
    at = row % HALF_LAT
    if col < HALF_LON:
        return 2 * WIDE + STRIP * upper + at * HALF_LON + col
    return WIDE * upper + at * (COLS - HALF_LON) + col - HALF_LON


def half_order(row, col):
    if col >= COLS:
        return LEVEL + piece_order(row, col - COLS) - 2 * WIDE
    return LEVEL // 2 * int(row < HALF_LAT) + (row % HALF_LAT) * COLS + col


def selection(shape, pairs):
    out = np.zeros(shape, np.float32)
    for row, column in pairs:
        out[row, column] = 1
    return jnp.asarray(out, BF16)


CELLS = list(np.ndindex(ROWS, COLS))
PLAIN = [(window_order(*cell), field_order(*cell)) for cell in CELLS]
JOIN = [(window_order(*cell), piece_order(*cell)) for cell in CELLS]
STRIPS = [(piece_order(*cell) - 2 * WIDE, field_order(*cell)) for cell in CELLS if cell[1] < HALF_LON]
SHIFTED = [((r + HALF_LAT) % ROWS, c + HALF_LON) for r, c in CELLS]
SHIFT = [(window_order(*cell), piece_order(r, c % COLS)) for cell, (r, c) in zip(CELLS, SHIFTED)]
SHIFT_HALF = [(window_order(*cell), half_order(r, c)) for cell, (r, c) in zip(CELLS, SHIFTED)]


def flipped(pairs):
    return [(column, row) for row, column in pairs]


class Fetched:
    def __init__(self, source, target, sem):
        self.copy, self.target, self.waiting = pltpu.make_async_copy(source, target, sem), target, True
        self.copy.start()

    def __getitem__(self, index):
        if self.waiting:
            self.copy.wait()
            self.waiting = False
        return self.target[index]


class Stored:
    def __init__(self, source, target, sem):
        self.copy, self.source = pltpu.make_async_copy(source, target, sem), source

    def __getitem__(self, index):
        return self.source[index]

    def __setitem__(self, index, value):
        self.source[index] = value

    def flush(self):
        self.copy.start()


def dot(a, b):
    return lax.dot_general(a, b, (((1,), (0,)), ((), ())), preferred_element_type=F32)


def dot_nt(a, b):
    return lax.dot_general(a, b, (((1,), (1,)), ((), ())), preferred_element_type=F32)


def dot_tn(a, b):
    return lax.dot_general(a, b, (((0,), (0,)), ((), ())), preferred_element_type=F32)


def gathered(matrix, levels):
    parts = [dot(matrix[...], level) for level in levels]
    segments = [part[w * SEGMENT : (w + 1) * SEGMENT] for w in range(WINDOWS) for part in parts]
    return jnp.concatenate(segments, axis=0)


def scattered(matrix, values):
    parts = []
    for level in range(LEVELS):
        starts = [w * WINDOW + level * SEGMENT for w in range(WINDOWS)]
        own = jnp.concatenate([values[start : start + SEGMENT] for start in starts], axis=0)
        parts.append(dot(matrix[...], own.astype(BF16)).astype(BF16))
    return parts


def pieces_of(refs, strip_at=0):
    out = []
    for level in range(LEVELS):
        strip_start = strip_at + level * STRIP
        spans = [slice(level * WIDE, (level + 1) * WIDE)] * 2 + [slice(strip_start, strip_start + STRIP)] * 2
        out.append(jnp.concatenate([ref[span] for ref, span in zip(refs, spans)], axis=0))
    return out


def put_pieces(parts, refs):
    for level, part in enumerate(parts):
        at = 0
        for ref, size in zip(refs, (WIDE, WIDE, STRIP, STRIP)):
            ref[level * size : (level + 1) * size] = part[at : at + size]
            at += size


def layer_norm(values):
    centred = values - jnp.mean(values, axis=-1, keepdims=True)
    inverse = lax.rsqrt(jnp.mean(centred * centred, axis=-1, keepdims=True) + EPSILON)
    return centred * inverse, inverse


def stacked(part, scale):
    lane = lax.broadcasted_iota(jnp.int32, (1, QUAD), 1) // HEAD_DIM
    wide = [part * jnp.where(lane == h, scale, 0.0).astype(BF16) for h in range(4)]
    return jnp.concatenate(wide, axis=0)


def unstacked(product):
    lane = lax.broadcasted_iota(jnp.int32, (WINDOW, QUAD), 1) // HEAD_DIM
    out = product[:WINDOW]
    for h in range(1, 4):
        out = jnp.where(lane == h, product[h * WINDOW : (h + 1) * WINDOW], out)
    return out


def soft(keys_stacked, queries, bias):
    scores = dot_nt(keys_stacked, queries).reshape(4, WINDOW, WINDOW)
    if bias is not None:
        scores = scores + bias[None]
    top = jnp.max(scores, axis=1, keepdims=True)
    raised = jnp.exp(scores - top)
    return raised * (1.0 / jnp.sum(raised, axis=1, keepdims=True))


def places(w, quad):
    span = slice(w * WINDOW, (w + 1) * WINDOW)
    return span, [slice(n * D + quad * QUAD, n * D + (quad + 1) * QUAD) for n in range(3)]


def forward_kernel(
    tokens, cotangent, w_qkv, w_proj, plain, cut, strips,
    keep, tall, side, corner, values_out, normed_out, packed, probs_out, mixed,
):
    values = gathered(plain, [tokens[:LEVEL], tokens[LEVEL:]])
    values_out[...] = values.astype(BF16)
    values_out.flush()
    normed = layer_norm(values)[0].astype(BF16)
    normed_out[...] = normed
    normed_out.flush()
    packed[...] = dot(normed, w_qkv[...]).astype(BF16)
    packed.flush()
    for w in range(WINDOWS):
        for quad in range(2):
            span, at = places(w, quad)
            queries, keys, vals = [packed[span, at[n]] for n in range(3)]
            probs = soft(stacked(keys, SCALE), queries, None).astype(BF16).reshape(4 * WINDOW, WINDOW)
            probs_out[2 * w + quad] = probs
            mixed[span, at[0]] = dot_tn(probs, stacked(vals, 1.0)).astype(BF16)
    probs_out.flush()
    mixed.flush()
    first = values + dot(mixed[...], w_proj[...])
    put_pieces(scattered(cut, first), (keep, tall, side, corner))
    for level in range(LEVELS):
        part = dot(strips[...], cotangent[level * LEVEL : (level + 1) * LEVEL]).astype(BF16)
        at = slice((LEVELS + level) * STRIP, (LEVELS + level + 1) * STRIP)
        side[at] = part[:STRIP]
        corner[at] = part[STRIP:]


def attention_backward(packed, probs, probs_low, d_mixed, d_packed, span, at, keys_stacked, vals_stacked):
    d_probs = dot_nt(vals_stacked, d_mixed).reshape(4, WINDOW, WINDOW)
    inner = jnp.sum(probs * d_probs, axis=1, keepdims=True)
    d_scores = (probs * (d_probs - inner)).astype(BF16).reshape(4 * WINDOW, WINDOW)
    d_packed[span, at[0]] = dot_tn(d_scores, keys_stacked).astype(BF16)
    d_packed[span, at[1]] = (unstacked(dot(d_scores, packed[span, at[0]])) * SCALE).astype(BF16)
    d_packed[span, at[2]] = unstacked(dot(probs_low, d_mixed)).astype(BF16)


def input_gradient(values, gradient, d_packed, w_qkv):
    standard, inverse = layer_norm(values)
    d_normed = dot_nt(d_packed, w_qkv)
    d_input = inverse * (
        d_normed
        - jnp.mean(d_normed, axis=-1, keepdims=True)
        - standard * jnp.mean(d_normed * standard, axis=-1, keepdims=True)
    )
    return gradient.astype(F32) + d_input


def weight_gradients(core, normed, d_packed, mixed, gradient, grads, kept, sent):
    grads[:, :48] = dot_tn(d_packed, normed).astype(BF16).reshape(32, 48, D)
    grads[:, 48:] = dot_tn(gradient, mixed).astype(BF16).reshape(32, 16, D)
    for j in range(16):
        kept[j] = grads[2 * j + core[0]]
        sent[j] = grads[2 * j + 1 - core[0]]


def shifted_kernel(
    core, keep, tall, side, corner, cotangent, tall_g, w_qkv, w_proj, gather, gather_g, scatter, bias,
    keep_out, tall_out, side_out, corner_out, kept, sent,
    packed, d_mixed_all, mixed, d_packed, grads,
):
    sources = []
    for level in range(LEVELS):
        own = cotangent[level * LEVEL + LEVEL // 2 : (level + 1) * LEVEL]
        beside = [ref[(LEVELS + level) * STRIP : (LEVELS + level + 1) * STRIP] for ref in (side, corner)]
        sources.append(
            jnp.concatenate([own, tall_g[level * (LEVEL // 2) : (level + 1) * (LEVEL // 2)], *beside], axis=0)
        )
    gradient = gathered(gather_g, sources).astype(BF16)
    d_mixed_all[...] = dot_nt(gradient, w_proj[...]).astype(BF16)
    values = gathered(gather, pieces_of((keep, tall, side, corner)))
    normed = layer_norm(values)[0].astype(BF16)
    packed[...] = dot(normed, w_qkv[...]).astype(BF16)
    for w in range(WINDOWS):
        for quad in range(2):
            span, at = places(w, quad)
            queries, keys, vals = [packed[span, at[n]] for n in range(3)]
            keys_stacked, vals_stacked = stacked(keys, SCALE), stacked(vals, 1.0)
            probs = soft(keys_stacked, queries, bias[...])
            probs_low = probs.astype(BF16).reshape(4 * WINDOW, WINDOW)
            mixed[span, at[0]] = dot_tn(probs_low, vals_stacked).astype(BF16)
            attention_backward(
                packed, probs, probs_low, d_mixed_all[span, at[0]], d_packed, span, at, keys_stacked, vals_stacked
            )
    weight_gradients(core, normed, d_packed[...], mixed[...], gradient, grads, kept, sent)
    kept.flush()
    sent.flush()
    result = input_gradient(values, gradient, d_packed[...], w_qkv[...])
    put_pieces(scattered(scatter, result), (keep_out, tall_out, side_out, corner_out))


def plain_kernel(
    core, keep, tall, side, corner, w_proj, join, packed, probs_in, mixed, normed, values, w_qkv, unplain,
    d_tokens, kept, sent,
    d_mixed_all, grads, d_packed,
):
    gradient = gathered(join, pieces_of((keep, tall, side, corner))).astype(BF16)
    d_mixed_all[...] = dot_nt(gradient, w_proj[...]).astype(BF16)
    for w in range(WINDOWS):
        for quad in range(2):
            span, at = places(w, quad)
            keys_stacked, vals_stacked = stacked(packed[span, at[1]], SCALE), stacked(packed[span, at[2]], 1.0)
            probs_low = probs_in[2 * w + quad]
            probs = probs_low.astype(F32).reshape(4, WINDOW, WINDOW)
            attention_backward(
                packed, probs, probs_low, d_mixed_all[span, at[0]], d_packed, span, at, keys_stacked, vals_stacked
            )
    weight_gradients(core, normed[...], d_packed[...], mixed[...], gradient, grads, kept, sent)
    kept.flush()
    sent.flush()
    result = input_gradient(values[...].astype(F32), gradient, d_packed[...], w_qkv[...])
    for level, part in enumerate(scattered(unplain, result)):
        d_tokens[level * LEVEL : (level + 1) * LEVEL] = part


def swapped_halves(top, bottom):
    left = lax.broadcasted_iota(jnp.int32, top.shape, 1) < top.shape[1] // 2
    turned = [pltpu.roll(x, top.shape[1] // 2, 1) for x in (top, bottom)]
    return jnp.where(left, top, turned[1]), jnp.where(left, turned[0], bottom)


def core_sums(kept, received):
    half = kept.shape[0] // 2
    for pair in range(4):
        at = slice(pair * 128, (pair + 1) * 128)
        total = kept[:, at].astype(F32) + received[:, at].astype(F32)
        for odd, part in enumerate(swapped_halves(total[:half], total[half:])):
            yield 2 * pair + odd, part.astype(BF16)


def core_sum_kernel(kept, received, out):
    for lat, part in core_sums(kept, received):
        out[lat] = part


def core_cut_kernel(place, kept, received, *refs):
    outs, held = refs[:-1], refs[-1]
    for lat, part in core_sums(kept, received):
        held[lat // 2, lat % 2] = part
    for step, out in enumerate(outs):
        out[...] = held[lax.rem(place[0] + step, 4)]


def far_sum_kernel(place, one, two, three, four, kept, sent):
    total = one[...].astype(F32) + two[...].astype(F32) + three[...].astype(F32) + four[...].astype(F32)
    first = place[0] == 0
    kept[...] = jnp.where(first, total[0], total[1]).astype(BF16)
    sent[...] = jnp.where(first, total[1], total[0]).astype(BF16)


def lat_sum_kernel(parts, kept, received, out):
    total = parts[0].astype(F32)
    for a in range(1, 8):
        total = total + parts[a].astype(F32)
    other = kept[...].astype(F32) + received[...].astype(F32)
    for block, held in enumerate((total, other)):
        for j in range(8):
            low, high = swapped_halves(held[64 * j : 64 * j + 32], held[64 * j + 32 : 64 * j + 64])
            out[j, block] = low.astype(BF16)
            out[j + 8, block] = high.astype(BF16)


def lon_sum_kernel(parts, grad_qkv, grad_proj):
    for block in range(2):
        total = parts[0, block].astype(F32)
        for j in range(1, 16):
            total = total + parts[j, block].astype(F32)
        whole = jnp.concatenate([total, pltpu.roll(total, 64, 1)], axis=0)
        grad_qkv[block] = whole[:48, :64]
        grad_proj[block] = whole[48:, :64]


def shape(*dims, kind=BF16):
    return jax.ShapeDtypeStruct(dims, kind)


def call(kernel, name, outs, *operands, scratch=(), scalar=False, fetch=None, store=(), limit=SMALL, micros=1):
    fetch = fetch or {}
    several = outs if isinstance(outs, tuple) else (outs,)
    cut = np.cumsum([0, len(operands), len(several), len(scratch), len(fetch), len(store)])

    def body(*refs):
        ins, results, own, landing, leaving = [list(refs[a:b]) for a, b in zip(cut[:-1], cut[1:])]
        for at, (n, index) in enumerate(fetch.items()):
            ins[n] = Fetched(ins[n] if index is None else ins[n].at[index], landing[at], refs[-2].at[at])
        for at, n in enumerate(store):
            results[n] = Stored(leaving[at], results[n], refs[-1].at[at])
        kernel(*ins, *results, *own)
        for n in store:
            results[n].copy.wait()

    held = [pltpu.VMEM(dims, BF16) for dims in scratch]
    for n, index in fetch.items():
        held.append(pltpu.VMEM(operands[n].shape if index is None else operands[n].shape[1:], BF16))
    held += [pltpu.VMEM(several[n].shape, BF16) for n in store]
    if fetch or store:
        held += [pltpu.SemaphoreType.DMA((max(1, len(group)),)) for group in (fetch, store)]
    kinds = [pltpu.HBM if n in fetch else pltpu.VMEM for n in range(len(operands))]
    if scalar:
        kinds[0] = pltpu.SMEM
    specs = tuple(pl.BlockSpec(memory_space=pltpu.HBM if n in store else pltpu.VMEM) for n in range(len(several)))
    return pl.pallas_call(
        body,
        out_shape=outs,
        in_specs=[pl.BlockSpec(memory_space=kind) for kind in kinds],
        out_specs=specs if isinstance(outs, tuple) else specs[0],
        scratch_shapes=held,
        compiler_params=pltpu.CompilerParams(vmem_limit_bytes=limit * 1024 * 1024),
        cost_estimate=pl.CostEstimate(
            flops=micros * PEAK_FLOPS, bytes_accessed=micros * PEAK_BYTES, transcendentals=0
        ),
        name=name,
    )(*operands)


def moved(piece, lat, lon):
    n_lat, n_lon = lax.axis_size("lat"), lax.axis_size("lon")
    if lon == 0:
        return lax.ppermute(piece, "lat", [(i, (i + lat) % n_lat) for i in range(n_lat)])
    if lat == 0:
        return lax.ppermute(piece, "lon", [(i, (i + lon) % n_lon) for i in range(n_lon)])
    route = [
        (a * n_lon + b, (a + lat) % n_lat * n_lon + (b + lon) % n_lon)
        for a in range(n_lat)
        for b in range(n_lon)
    ]
    return lax.ppermute(piece, ("lat", "lon"), route)


def exchanged(tall, side, corner, step):
    return moved(tall, step, 0), moved(side, 0, step), moved(corner, step, step)


def core_swapped(sent):
    return lax.ppermute(sent, "lon", [(i, i ^ 1) for i in range(lax.axis_size("lon"))]).reshape(1024, D)


def core_reduced(kept, sent):
    return call(core_sum_kernel, "core_sum", shape(8, 512, 128), kept.reshape(1024, D), core_swapped(sent), limit=12)


def core_cut(kept, sent):
    place = (lax.axis_index("lat") // 2).astype(jnp.int32).reshape(1)
    return call(
        core_cut_kernel, "core_cut", (shape(2, 512, 128),) * 4, place, kept.reshape(1024, D), core_swapped(sent),
        scratch=[(4, 2, 512, 128)], scalar=True, limit=12,
    )


def far_reduced(parts):
    n = lax.axis_size("lat")
    arrived = [parts[0]]
    for step in (2, 3, 1):
        arrived.append(lax.ppermute(parts[step], "lat", [(i, (i + 2 * step) % n) for i in range(n)]))
    place = (lax.axis_index("lat") % 2).astype(jnp.int32).reshape(1)
    kept, sent = call(far_sum_kernel, "far_sum", (shape(512, 128),) * 2, place, *arrived, scalar=True)
    return kept, sent


def reduced(chunks_one, parts_two):
    kept, sent = parts_two
    received = lax.ppermute(sent, "lat", [(i, i ^ 1) for i in range(lax.axis_size("lat"))])
    arrived = lax.all_to_all(chunks_one, "lat", 0, 0, tiled=True)
    both = call(lat_sum_kernel, "lat_sum", shape(16, 2, 32, 128), arrived, kept, received)
    groups = [[2 * j + core for j in range(16)] for core in range(2)]
    arrived = lax.all_to_all(both, "lon", 0, 0, tiled=True, axis_index_groups=groups)
    grads = call(lon_sum_kernel, "lon_sum", (shape(2, 48, 64, kind=F32), shape(2, 16, 64, kind=F32)), arrived)
    return [grad.transpose(0, 2, 1) for grad in grads]


def body(tokens, cotangent, qkv_weights, proj_weights):
    plain, unplain = selection((LEVEL, LEVEL), PLAIN), selection((LEVEL, LEVEL), flipped(PLAIN))
    join, cut = selection((LEVEL, PIECES), JOIN), selection((PIECES, LEVEL), flipped(JOIN))
    shift, unshift = selection((LEVEL, PIECES), SHIFT), selection((PIECES, LEVEL), flipped(SHIFT))
    shift_half, strips = selection((LEVEL, LEVEL + 2 * STRIP), SHIFT_HALF), selection((2 * STRIP, LEVEL), STRIPS)
    core = (lax.axis_index("lon") % 2).astype(jnp.int32).reshape(1)
    last_lat = lax.axis_index("lat") == lax.axis_size("lat") - 1
    label = (np.arange(WINDOW) // WIN_LON % WIN_LAT >= HALF_LAT).astype(np.int32)
    bias = jnp.where(last_lat & (label[:, None] != label[None, :]), MASKED, 0.0).astype(F32)
    field, flat = shape(TOKENS, D), tokens.reshape(TOKENS, D)
    wide, strip, pair = [shape(LEVELS * rows, D) for rows in (WIDE, STRIP, 2 * STRIP)]
    packed_field = shape(TOKENS, 3 * D)
    half = shape(16, 64, D)

    tall_g = moved(cotangent[:, :HALF_LAT].reshape(HALF, D), -1, 0)
    flat_g = cotangent.reshape(TOKENS, D)
    keep, tall, side, corner, values, normed, packed, probs, mixed = call(
        forward_kernel,
        "forward",
        (wide, wide, pair, pair, field, field, packed_field, shape(2 * WINDOWS, 4 * WINDOW, WINDOW), field),
        flat, flat_g, qkv_weights, proj_weights, plain, cut, strips,
        fetch={4: None, 0: None, 2: 0, 3: 0, 5: None, 6: None, 1: None},
        store=(4, 5, 6, 7, 8),
        limit=LARGE,
        micros=9,
    )
    tall, side, corner = exchanged(tall, side, corner, -1)
    keep, tall, side, corner, kept_two, sent_two = call(
        shifted_kernel,
        "backward_shifted",
        (wide, wide, strip, strip, half, half),
        core, keep, tall, side, corner, flat_g, tall_g, qkv_weights, proj_weights, shift, shift_half, unshift, bias,
        scratch=[(TOKENS, 3 * D), (TOKENS, D), (TOKENS, D), (TOKENS, 3 * D), (32, 64, D)],
        scalar=True,
        fetch={5: None, 10: None, 8: 1, 9: None, 7: 1, 11: None},
        store=(4, 5),
        limit=LARGE,
        micros=18,
    )
    tall, side, corner = exchanged(tall, side, corner, 1)
    parts_two = far_reduced(core_cut(kept_two, sent_two))
    d_tokens, kept_one, sent_one = call(
        plain_kernel,
        "backward_plain",
        (field, half, half),
        core, keep, tall, side, corner, proj_weights, join, packed, probs, mixed, normed, values, qkv_weights, unplain,
        scratch=[(TOKENS, D), (32, 64, D), (TOKENS, 3 * D)],
        scalar=True,
        fetch={6: None, 5: 0, 7: None, 8: None, 10: None, 9: None, 12: 0, 11: None, 13: None},
        store=(1, 2),
        limit=LARGE,
        micros=13,
    )
    sent_one, parts_two = lax.optimization_barrier((sent_one, parts_two))
    grad_qkv, grad_proj = reduced(core_reduced(kept_one, sent_one), parts_two)
    return d_tokens.reshape(tokens.shape), grad_qkv, grad_proj


def solution(mesh):
    return jax.shard_map(
        body,
        mesh=mesh,
        in_specs=(P(None, "lat", "lon", None), P(None, "lat", "lon", None), P(), P()),
        out_specs=(P(None, "lat", "lon", None), P(None, "lat", "lon"), P(None, "lat", "lon")),
        check_vma=False,
    )
```

```python
import functools

import jax
import jax.numpy as jnp
import numpy as np
from jax import lax
from jax.experimental import pallas as pl
from jax.experimental.pallas import tpu as pltpu
from jax.sharding import PartitionSpec as P

D = 512
HEADS = 8
HEAD_DIM = 64
LEVELS = 2
WIN_LAT = 12
WIN_LON = 6
HALF_LAT = 6
HALF_LON = 3
ROWS = 12
COLS = 24
TOKENS = LEVELS * ROWS * COLS
WINDOW = LEVELS * WIN_LAT * WIN_LON
WINDOWS = TOKENS // WINDOW
HALF = TOKENS // 2
QUAD = 4 * HEAD_DIM
LEVEL = ROWS * COLS
SEGMENT = WIN_LAT * WIN_LON
WIDE = 128
STRIP = 32
PIECES = 2 * WIDE + 2 * STRIP
EPSILON = 1e-05
MASKED = -1000000000.0
SCALE = HEAD_DIM ** (-0.5)
LARGE = 58
SMALL = 6
PEAK_FLOPS = 1_150_000_000
PEAK_BYTES = 3_690_000
F32 = jnp.float32
BF16 = jnp.bfloat16


def window_order(row, col):
    return (col // WIN_LON) * SEGMENT + row * WIN_LON + col % WIN_LON


def field_order(row, col):
    return row * COLS + col


def piece_order(row, col):
    upper = int(row < HALF_LAT)
    at = row % HALF_LAT
    if col < HALF_LON:
        return 2 * WIDE + STRIP * upper + at * HALF_LON + col
    return WIDE * upper + at * (COLS - HALF_LON) + col - HALF_LON


def half_order(row, col):
    if col >= COLS:
        return LEVEL + piece_order(row, col - COLS) - 2 * WIDE
    return LEVEL // 2 * int(row < HALF_LAT) + (row % HALF_LAT) * COLS + col


def selection(shape, pairs):
    out = np.zeros(shape, np.float32)
    for row, column in pairs:
        out[row, column] = 1
    return jnp.asarray(out, BF16)


CELLS = list(np.ndindex(ROWS, COLS))
PLAIN = [(window_order(*cell), field_order(*cell)) for cell in CELLS]
JOIN = [(window_order(*cell), piece_order(*cell)) for cell in CELLS]
STRIPS = [(piece_order(*cell) - 2 * WIDE, field_order(*cell)) for cell in CELLS if cell[1] < HALF_LON]
SHIFTED = [((r + HALF_LAT) % ROWS, c + HALF_LON) for r, c in CELLS]
SHIFT = [(window_order(*cell), piece_order(r, c % COLS)) for cell, (r, c) in zip(CELLS, SHIFTED)]
SHIFT_HALF = [(window_order(*cell), half_order(r, c)) for cell, (r, c) in zip(CELLS, SHIFTED)]


def flipped(pairs):
    return [(column, row) for row, column in pairs]


class Fetched:
    def __init__(self, source, target, sem):
        self.copy, self.target, self.waiting = pltpu.make_async_copy(source, target, sem), target, True
        self.copy.start()

    def __getitem__(self, index):
        if self.waiting:
            self.copy.wait()
            self.waiting = False
        return self.target[index]


class Stored:
    def __init__(self, source, target, sem):
        self.copy, self.source = pltpu.make_async_copy(source, target, sem), source

    def __getitem__(self, index):
        return self.source[index]

    def __setitem__(self, index, value):
        self.source[index] = value

    def flush(self):
        self.copy.start()


def dot(a, b):
    return lax.dot_general(a, b, (((1,), (0,)), ((), ())), preferred_element_type=F32)


def dot_nt(a, b):
    return lax.dot_general(a, b, (((1,), (1,)), ((), ())), preferred_element_type=F32)


def dot_tn(a, b):
    return lax.dot_general(a, b, (((0,), (0,)), ((), ())), preferred_element_type=F32)


def gathered(matrix, levels):
    parts = [dot(matrix[...], level) for level in levels]
    segments = [part[w * SEGMENT : (w + 1) * SEGMENT] for w in range(WINDOWS) for part in parts]
    return jnp.concatenate(segments, axis=0)


def scattered(matrix, values):
    parts = []
    for level in range(LEVELS):
        starts = [w * WINDOW + level * SEGMENT for w in range(WINDOWS)]
        own = jnp.concatenate([values[start : start + SEGMENT] for start in starts], axis=0)
        parts.append(dot(matrix[...], own.astype(BF16)).astype(BF16))
    return parts


def pieces_of(refs, strip_at=0):
    out = []
    for level in range(LEVELS):
        strip_start = strip_at + level * STRIP
        spans = [slice(level * WIDE, (level + 1) * WIDE)] * 2 + [slice(strip_start, strip_start + STRIP)] * 2
        out.append(jnp.concatenate([ref[span] for ref, span in zip(refs, spans)], axis=0))
    return out


def put_pieces(parts, refs):
    for level, part in enumerate(parts):
        at = 0
        for ref, size in zip(refs, (WIDE, WIDE, STRIP, STRIP)):
            ref[level * size : (level + 1) * size] = part[at : at + size]
            at += size


def layer_norm(values):
    centred = values - jnp.mean(values, axis=-1, keepdims=True)
    inverse = lax.rsqrt(jnp.mean(centred * centred, axis=-1, keepdims=True) + EPSILON)
    return centred * inverse, inverse


def stacked(part, scale):
    lane = lax.broadcasted_iota(jnp.int32, (1, QUAD), 1) // HEAD_DIM
    wide = [part * jnp.where(lane == h, scale, 0.0).astype(BF16) for h in range(4)]
    return jnp.concatenate(wide, axis=0)


def unstacked(product):
    lane = lax.broadcasted_iota(jnp.int32, (WINDOW, QUAD), 1) // HEAD_DIM
    out = product[:WINDOW]
    for h in range(1, 4):
        out = jnp.where(lane == h, product[h * WINDOW : (h + 1) * WINDOW], out)
    return out


def soft(keys_stacked, queries, bias):
    out = []
    for h in range(4):
        scores = dot_nt(keys_stacked[h * WINDOW : (h + 1) * WINDOW], queries)
        if bias is not None:
            scores = scores + bias
        raised = jnp.exp(scores - jnp.max(scores, axis=0, keepdims=True))
        out.append(raised * (1.0 / jnp.sum(raised, axis=0, keepdims=True)))
    return out


def places(w, quad):
    span = slice(w * WINDOW, (w + 1) * WINDOW)
    return span, [slice(n * D + quad * QUAD, n * D + (quad + 1) * QUAD) for n in range(3)]


def forward_kernel(
    tokens, cotangent, w_qkv, w_proj, plain, cut, strips,
    keep, tall, side, corner, values_out, normed_out, packed, probs_out, mixed,
):
    values = gathered(plain, [tokens[:LEVEL], tokens[LEVEL:]])
    values_out[...] = values.astype(BF16)
    values_out.flush()
    normed = layer_norm(values)[0].astype(BF16)
    normed_out[...] = normed
    normed_out.flush()
    packed[...] = dot(normed, w_qkv[...]).astype(BF16)
    packed.flush()
    for w in range(WINDOWS):
        for quad in range(2):
            span, at = places(w, quad)
            queries, keys, vals = [packed[span, at[n]] for n in range(3)]
            probs = jnp.concatenate(soft(stacked(keys, SCALE), queries, None), axis=0).astype(BF16)
            probs_out[2 * w + quad] = probs
            mixed[span, at[0]] = dot_tn(probs, stacked(vals, 1.0)).astype(BF16)
    probs_out.flush()
    mixed.flush()
    first = values + dot(mixed[...], w_proj[...])
    put_pieces(scattered(cut, first), (keep, tall, side, corner))
    for level in range(LEVELS):
        part = dot(strips[...], cotangent[level * LEVEL : (level + 1) * LEVEL]).astype(BF16)
        at = slice((LEVELS + level) * STRIP, (LEVELS + level + 1) * STRIP)
        side[at] = part[:STRIP]
        corner[at] = part[STRIP:]


def attention_backward(packed, probs, probs_low, d_mixed, d_packed, span, at, keys_stacked, vals_stacked):
    d_scores = []
    for h in range(4):
        d_probs = dot_nt(vals_stacked[h * WINDOW : (h + 1) * WINDOW], d_mixed)
        inner = jnp.sum(probs[h] * d_probs, axis=0, keepdims=True)
        d_scores.append((probs[h] * (d_probs - inner)).astype(BF16))
    d_scores = jnp.concatenate(d_scores, axis=0)
    d_packed[span, at[0]] = dot_tn(d_scores, keys_stacked).astype(BF16)
    d_packed[span, at[1]] = (unstacked(dot(d_scores, packed[span, at[0]])) * SCALE).astype(BF16)
    d_packed[span, at[2]] = unstacked(dot(probs_low, d_mixed)).astype(BF16)


def input_gradient(values, gradient, d_packed, w_qkv):
    standard, inverse = layer_norm(values)
    d_normed = dot_nt(d_packed, w_qkv)
    d_input = inverse * (
        d_normed
        - jnp.mean(d_normed, axis=-1, keepdims=True)
        - standard * jnp.mean(d_normed * standard, axis=-1, keepdims=True)
    )
    return gradient.astype(F32) + d_input


def weight_gradients(core, normed, d_packed, mixed, gradient, grads, kept, sent):
    grads[:, :48] = dot_tn(d_packed, normed).astype(BF16).reshape(32, 48, D)
    grads[:, 48:] = dot_tn(gradient, mixed).astype(BF16).reshape(32, 16, D)
    for j in range(16):
        kept[j] = grads[2 * j + core[0]]
        sent[j] = grads[2 * j + 1 - core[0]]


def shifted_kernel(
    core, keep, tall, side, corner, cotangent, tall_g, w_qkv, w_proj, gather, gather_g, scatter, bias,
    keep_out, tall_out, side_out, corner_out, kept, sent,
    packed, d_mixed_all, mixed, d_packed, grads,
):
    sources = []
    for level in range(LEVELS):
        own = cotangent[level * LEVEL + LEVEL // 2 : (level + 1) * LEVEL]
        beside = [ref[(LEVELS + level) * STRIP : (LEVELS + level + 1) * STRIP] for ref in (side, corner)]
        sources.append(
            jnp.concatenate([own, tall_g[level * (LEVEL // 2) : (level + 1) * (LEVEL // 2)], *beside], axis=0)
        )
    gradient = gathered(gather_g, sources).astype(BF16)
    d_mixed_all[...] = dot_nt(gradient, w_proj[...]).astype(BF16)
    values = gathered(gather, pieces_of((keep, tall, side, corner)))
    normed = layer_norm(values)[0].astype(BF16)
    packed[...] = dot(normed, w_qkv[...]).astype(BF16)
    for w in range(WINDOWS):
        for quad in range(2):
            span, at = places(w, quad)
            queries, keys, vals = [packed[span, at[n]] for n in range(3)]
            keys_stacked, vals_stacked = stacked(keys, SCALE), stacked(vals, 1.0)
            probs = soft(keys_stacked, queries, bias[...])
            probs_low = jnp.concatenate(probs, axis=0).astype(BF16)
            mixed[span, at[0]] = dot_tn(probs_low, vals_stacked).astype(BF16)
            attention_backward(
                packed, probs, probs_low, d_mixed_all[span, at[0]], d_packed, span, at, keys_stacked, vals_stacked
            )
    weight_gradients(core, normed, d_packed[...], mixed[...], gradient, grads, kept, sent)
    kept.flush()
    sent.flush()
    result = input_gradient(values, gradient, d_packed[...], w_qkv[...])
    put_pieces(scattered(scatter, result), (keep_out, tall_out, side_out, corner_out))


def plain_kernel(
    core, keep, tall, side, corner, w_proj, join, packed, probs_in, mixed, normed,
    gradient_out, d_packed, kept, sent,
    d_mixed_all, grads,
):
    gradient = gathered(join, pieces_of((keep, tall, side, corner))).astype(BF16)
    gradient_out[...] = gradient
    gradient_out.flush()
    d_mixed_all[...] = dot_nt(gradient, w_proj[...]).astype(BF16)
    for w in range(WINDOWS):
        for quad in range(2):
            span, at = places(w, quad)
            keys_stacked, vals_stacked = stacked(packed[span, at[1]], SCALE), stacked(packed[span, at[2]], 1.0)
            probs_low = probs_in[2 * w + quad]
            probs = [probs_low[h * WINDOW : (h + 1) * WINDOW].astype(F32) for h in range(4)]
            attention_backward(
                packed, probs, probs_low, d_mixed_all[span, at[0]], d_packed, span, at, keys_stacked, vals_stacked
            )
    d_packed.flush()
    weight_gradients(core, normed[...], d_packed[...], mixed[...], gradient, grads, kept, sent)
    kept.flush()
    sent.flush()


def finish_kernel(values, gradient, d_packed, w_qkv, unplain, d_tokens):
    result = input_gradient(values[...].astype(F32), gradient[...], d_packed[...], w_qkv[...])
    for level, part in enumerate(scattered(unplain, result)):
        d_tokens[level * LEVEL : (level + 1) * LEVEL] = part


def swapped_halves(top, bottom):
    left = lax.broadcasted_iota(jnp.int32, top.shape, 1) < top.shape[1] // 2
    turned = [pltpu.roll(x, top.shape[1] // 2, 1) for x in (top, bottom)]
    return jnp.where(left, top, turned[1]), jnp.where(left, turned[0], bottom)


def core_sums(kept, received, landing, sems):
    half = kept.shape[0] // 2
    spans = [slice(pair * 128, (pair + 1) * 128) for pair in range(4)]
    copies = [pltpu.make_async_copy(kept.at[:, at], landing.at[n], sems.at[n]) for n, at in enumerate(spans)]
    for copy in copies:
        copy.start()
    for pair, at in enumerate(spans):
        copies[pair].wait()
        total = landing[pair].astype(F32) + received[:, at].astype(F32)
        for odd, part in enumerate(swapped_halves(total[:half], total[half:])):
            yield 2 * pair + odd, part.astype(BF16)


def core_sum_kernel(kept, received, out, landing, made, sems):
    leaving = []
    for lat, part in core_sums(kept, received, landing, sems):
        made[lat] = part
        leaving.append(pltpu.make_async_copy(made.at[lat], out.at[lat], sems.at[4 + lat]))
        leaving[-1].start()
    for copy in leaving:
        copy.wait()


def core_cut_kernel(place, kept, received, *refs):
    outs, (landing, held, sems) = refs[:-3], refs[-3:]
    for lat, part in core_sums(kept, received, landing, sems):
        held[lat // 2, lat % 2] = part
    for step, out in enumerate(outs):
        out[...] = held[lax.rem(place[0] + step, 4)]


def far_sum_kernel(place, one, two, three, four, kept, sent):
    total = one[...].astype(F32) + two[...].astype(F32) + three[...].astype(F32) + four[...].astype(F32)
    first = place[0] == 0
    kept[...] = jnp.where(first, total[0], total[1]).astype(BF16)
    sent[...] = jnp.where(first, total[1], total[0]).astype(BF16)


def lat_sum_kernel(parts, kept, received, out):
    total = parts[0].astype(F32)
    for a in range(1, 8):
        total = total + parts[a].astype(F32)
    other = kept[...].astype(F32) + received[...].astype(F32)
    for block, held in enumerate((total, other)):
        for j in range(8):
            low, high = swapped_halves(held[64 * j : 64 * j + 32], held[64 * j + 32 : 64 * j + 64])
            out[j, block] = low.astype(BF16)
            out[j + 8, block] = high.astype(BF16)


def lon_sum_kernel(parts, grad_qkv, grad_proj):
    for block in range(2):
        total = parts[0, block].astype(F32)
        for j in range(1, 16):
            total = total + parts[j, block].astype(F32)
        whole = jnp.concatenate([total, pltpu.roll(total, 64, 1)], axis=0)
        grad_qkv[block] = whole[:48, :64]
        grad_proj[block] = whole[48:, :64]


def shape(*dims, kind=BF16):
    return jax.ShapeDtypeStruct(dims, kind)


def call(kernel, name, outs, *operands, scratch=(), scalar=False, fetch=None, store=(), apart=(), own_out=False, limit=SMALL, micros=1):
    fetch = fetch or {}
    several = outs if isinstance(outs, tuple) else (outs,)
    cut = np.cumsum([0, len(operands), len(several), len(scratch), len(fetch), len(store)])

    def body(*refs):
        ins, results, own, landing, leaving = [list(refs[a:b]) for a, b in zip(cut[:-1], cut[1:])]
        for at, (n, index) in enumerate(fetch.items()):
            ins[n] = Fetched(ins[n] if index is None else ins[n].at[index], landing[at], refs[-2].at[at])
        for at, n in enumerate(store):
            results[n] = Stored(leaving[at], results[n], refs[-1].at[at])
        kernel(*ins, *results, *own)
        for n in store:
            results[n].copy.wait()

    held = [pltpu.VMEM(dims, BF16) if isinstance(dims, tuple) else dims for dims in scratch]
    for n, index in fetch.items():
        held.append(pltpu.VMEM(operands[n].shape if index is None else operands[n].shape[1:], BF16))
    held += [pltpu.VMEM(several[n].shape, BF16) for n in store]
    if fetch or store:
        held += [pltpu.SemaphoreType.DMA((max(1, len(group)),)) for group in (fetch, store)]
    kinds = [pltpu.HBM if n in fetch or n in apart else pltpu.VMEM for n in range(len(operands))]
    if scalar:
        kinds[0] = pltpu.SMEM
    specs = tuple(pl.BlockSpec(memory_space=pltpu.HBM if own_out or n in store else pltpu.VMEM) for n in range(len(several)))
    return pl.pallas_call(
        body,
        out_shape=outs,
        in_specs=[pl.BlockSpec(memory_space=kind) for kind in kinds],
        out_specs=specs if isinstance(outs, tuple) else specs[0],
        scratch_shapes=held,
        compiler_params=pltpu.CompilerParams(vmem_limit_bytes=limit * 1024 * 1024),
        cost_estimate=pl.CostEstimate(
            flops=micros * PEAK_FLOPS, bytes_accessed=micros * PEAK_BYTES, transcendentals=0
        ),
        name=name,
    )(*operands)


def moved(piece, lat, lon):
    n_lat, n_lon = lax.axis_size("lat"), lax.axis_size("lon")
    if lon == 0:
        return lax.ppermute(piece, "lat", [(i, (i + lat) % n_lat) for i in range(n_lat)])
    if lat == 0:
        return lax.ppermute(piece, "lon", [(i, (i + lon) % n_lon) for i in range(n_lon)])
    route = [
        (a * n_lon + b, (a + lat) % n_lat * n_lon + (b + lon) % n_lon)
        for a in range(n_lat)
        for b in range(n_lon)
    ]
    return lax.ppermute(piece, ("lat", "lon"), route)


def exchanged(tall, side, corner, step):
    return moved(tall, step, 0), moved(side, 0, step), moved(corner, step, step)


def core_swapped(sent):
    return lax.ppermute(sent, "lon", [(i, i ^ 1) for i in range(lax.axis_size("lon"))]).reshape(1024, D)


def core_reduced(kept, sent):
    return call(
        core_sum_kernel, "core_sum", shape(8, 512, 128), kept.reshape(1024, D), core_swapped(sent),
        scratch=[(4, 1024, 128), (8, 512, 128), pltpu.SemaphoreType.DMA((12,))], apart=(0,), own_out=True, limit=12,
    )


def core_cut(kept, sent):
    place = (lax.axis_index("lat") // 2).astype(jnp.int32).reshape(1)
    return call(
        core_cut_kernel, "core_cut", (shape(2, 512, 128),) * 4, place, kept.reshape(1024, D), core_swapped(sent),
        scratch=[(4, 1024, 128), (4, 2, 512, 128), pltpu.SemaphoreType.DMA((4,))], scalar=True, apart=(1,), limit=12,
    )


def far_reduced(parts):
    n = lax.axis_size("lat")
    arrived = [parts[0]]
    for step in (2, 3, 1):
        arrived.append(lax.ppermute(parts[step], "lat", [(i, (i + 2 * step) % n) for i in range(n)]))
    place = (lax.axis_index("lat") % 2).astype(jnp.int32).reshape(1)
    kept, sent = call(far_sum_kernel, "far_sum", (shape(512, 128),) * 2, place, *arrived, scalar=True)
    return kept, sent


def reduced(chunks_one, parts_two):
    kept, sent = parts_two
    received = lax.ppermute(sent, "lat", [(i, i ^ 1) for i in range(lax.axis_size("lat"))])
    arrived = lax.all_to_all(chunks_one, "lat", 0, 0, tiled=True)
    both = call(lat_sum_kernel, "lat_sum", shape(16, 2, 32, 128), arrived, kept, received)
    groups = [[2 * j + core for j in range(16)] for core in range(2)]
    arrived = lax.all_to_all(both, "lon", 0, 0, tiled=True, axis_index_groups=groups)
    grads = call(lon_sum_kernel, "lon_sum", (shape(2, 48, 64, kind=F32), shape(2, 16, 64, kind=F32)), arrived)
    return [grad.transpose(0, 2, 1) for grad in grads]


def body(tokens, cotangent, qkv_weights, proj_weights):
    plain, unplain = selection((LEVEL, LEVEL), PLAIN), selection((LEVEL, LEVEL), flipped(PLAIN))
    join, cut = selection((LEVEL, PIECES), JOIN), selection((PIECES, LEVEL), flipped(JOIN))
    shift, unshift = selection((LEVEL, PIECES), SHIFT), selection((PIECES, LEVEL), flipped(SHIFT))
    shift_half, strips = selection((LEVEL, LEVEL + 2 * STRIP), SHIFT_HALF), selection((2 * STRIP, LEVEL), STRIPS)
    core = (lax.axis_index("lon") % 2).astype(jnp.int32).reshape(1)
    last_lat = lax.axis_index("lat") == lax.axis_size("lat") - 1
    label = (np.arange(WINDOW) // WIN_LON % WIN_LAT >= HALF_LAT).astype(np.int32)
    bias = jnp.where(last_lat & (label[:, None] != label[None, :]), MASKED, 0.0).astype(F32)
    field, flat = shape(TOKENS, D), tokens.reshape(TOKENS, D)
    wide, strip, pair = [shape(LEVELS * rows, D) for rows in (WIDE, STRIP, 2 * STRIP)]
    packed_field = shape(TOKENS, 3 * D)
    half = shape(16, 64, D)

    tall_g = moved(cotangent[:, :HALF_LAT].reshape(HALF, D), -1, 0)
    flat_g = cotangent.reshape(TOKENS, D)
    keep, tall, side, corner, values, normed, packed, probs, mixed = call(
        forward_kernel,
        "forward",
        (wide, wide, pair, pair, field, field, packed_field, shape(2 * WINDOWS, 4 * WINDOW, WINDOW), field),
        flat, flat_g, qkv_weights, proj_weights, plain, cut, strips,
        fetch={4: None, 0: None, 2: 0, 3: 0, 5: None, 6: None, 1: None},
        store=(4, 5, 6, 7, 8),
        limit=LARGE,
        micros=9,
    )
    tall, side, corner = exchanged(tall, side, corner, -1)
    keep, tall, side, corner, kept_two, sent_two = call(
        shifted_kernel,
        "backward_shifted",
        (wide, wide, strip, strip, half, half),
        core, keep, tall, side, corner, flat_g, tall_g, qkv_weights, proj_weights, shift, shift_half, unshift, bias,
        scratch=[(TOKENS, 3 * D), (TOKENS, D), (TOKENS, D), (TOKENS, 3 * D), (32, 64, D)],
        scalar=True,
        fetch={5: None, 10: None, 8: 1, 9: None, 7: 1, 11: None},
        store=(4, 5),
        limit=LARGE,
        micros=18,
    )
    tall, side, corner = exchanged(tall, side, corner, 1)
    parts_two = far_reduced(core_cut(kept_two, sent_two))
    gradient, d_packed, kept_one, sent_one = call(
        plain_kernel,
        "backward_plain",
        (field, packed_field, half, half),
        core, keep, tall, side, corner, proj_weights, join, packed, probs, mixed, normed,
        scratch=[(TOKENS, D), (32, 64, D)],
        scalar=True,
        fetch={6: None, 5: 0, 7: None, 8: None, 10: None, 9: None},
        store=(0, 1, 2, 3),
        limit=LARGE,
        micros=10,
    )
    d_tokens = call(
        finish_kernel,
        "finish_plain",
        field,
        values, gradient, d_packed, qkv_weights, unplain,
        fetch={2: None, 3: 0, 0: None, 1: None, 4: None},
        limit=LARGE,
        micros=5,
    )
    sent_one, parts_two = lax.optimization_barrier((sent_one, parts_two))
    grad_qkv, grad_proj = reduced(core_reduced(kept_one, sent_one), parts_two)
    return d_tokens.reshape(tokens.shape), grad_qkv, grad_proj


def solution(mesh):
    return jax.shard_map(
        body,
        mesh=mesh,
        in_specs=(P(None, "lat", "lon", None), P(None, "lat", "lon", None), P(), P()),
        out_specs=(P(None, "lat", "lon", None), P(None, "lat", "lon"), P(None, "lat", "lon")),
        check_vma=False,
    )
```

```python
import functools

import jax
import jax.numpy as jnp
import numpy as np
from jax import lax
from jax.experimental import pallas as pl
from jax.experimental.pallas import tpu as pltpu
from jax.sharding import PartitionSpec as P

D = 512
HEADS = 8
HEAD_DIM = 64
LEVELS = 2
WIN_LAT = 12
WIN_LON = 6
HALF_LAT = 6
HALF_LON = 3
ROWS = 12
COLS = 24
TOKENS = LEVELS * ROWS * COLS
WINDOW = LEVELS * WIN_LAT * WIN_LON
WINDOWS = TOKENS // WINDOW
HALF = TOKENS // 2
QUAD = 4 * HEAD_DIM
LEVEL = ROWS * COLS
SEGMENT = WIN_LAT * WIN_LON
WIDE = 128
STRIP = 32
PIECES = 2 * WIDE + 2 * STRIP
EPSILON = 1e-05
MASKED = -1000000000.0
SCALE = HEAD_DIM ** (-0.5)
LARGE = 58
SMALL = 6
PEAK_FLOPS = 1_150_000_000
PEAK_BYTES = 3_690_000
F32 = jnp.float32
BF16 = jnp.bfloat16


def window_order(row, col):
    return (col // WIN_LON) * SEGMENT + row * WIN_LON + col % WIN_LON


def field_order(row, col):
    return row * COLS + col


def piece_order(row, col):
    upper = int(row < HALF_LAT)
    at = row % HALF_LAT
    if col < HALF_LON:
        return 2 * WIDE + STRIP * upper + at * HALF_LON + col
    return WIDE * upper + at * (COLS - HALF_LON) + col - HALF_LON


def half_order(row, col):
    if col >= COLS:
        return LEVEL + piece_order(row, col - COLS) - 2 * WIDE
    return LEVEL // 2 * int(row < HALF_LAT) + (row % HALF_LAT) * COLS + col


def selection(shape, pairs):
    out = np.zeros(shape, np.float32)
    for row, column in pairs:
        out[row, column] = 1
    return jnp.asarray(out, BF16)


CELLS = list(np.ndindex(ROWS, COLS))
PLAIN = [(window_order(*cell), field_order(*cell)) for cell in CELLS]
JOIN = [(window_order(*cell), piece_order(*cell)) for cell in CELLS]
STRIPS = [(piece_order(*cell) - 2 * WIDE, field_order(*cell)) for cell in CELLS if cell[1] < HALF_LON]
SHIFTED = [((r + HALF_LAT) % ROWS, c + HALF_LON) for r, c in CELLS]
SHIFT = [(window_order(*cell), piece_order(r, c % COLS)) for cell, (r, c) in zip(CELLS, SHIFTED)]
SHIFT_HALF = [(window_order(*cell), half_order(r, c)) for cell, (r, c) in zip(CELLS, SHIFTED)]


def flipped(pairs):
    return [(column, row) for row, column in pairs]


class Fetched:
    def __init__(self, source, target, sem):
        self.copy, self.target, self.waiting = pltpu.make_async_copy(source, target, sem), target, True
        self.copy.start()

    def __getitem__(self, index):
        if self.waiting:
            self.copy.wait()
            self.waiting = False
        return self.target[index]


class Stored:
    def __init__(self, source, target, sem):
        self.copy, self.source = pltpu.make_async_copy(source, target, sem), source

    def __getitem__(self, index):
        return self.source[index]

    def __setitem__(self, index, value):
        self.source[index] = value

    def flush(self):
        self.copy.start()


def dot(a, b):
    return lax.dot_general(a, b, (((1,), (0,)), ((), ())), preferred_element_type=F32)


def dot_nt(a, b):
    return lax.dot_general(a, b, (((1,), (1,)), ((), ())), preferred_element_type=F32)


def dot_tn(a, b):
    return lax.dot_general(a, b, (((0,), (0,)), ((), ())), preferred_element_type=F32)


def gathered(matrix, levels):
    parts = [dot(matrix[...], level) for level in levels]
    segments = [part[w * SEGMENT : (w + 1) * SEGMENT] for w in range(WINDOWS) for part in parts]
    return jnp.concatenate(segments, axis=0)


def scattered(matrix, values):
    parts = []
    for level in range(LEVELS):
        starts = [w * WINDOW + level * SEGMENT for w in range(WINDOWS)]
        own = jnp.concatenate([values[start : start + SEGMENT] for start in starts], axis=0)
        parts.append(dot(matrix[...], own.astype(BF16)).astype(BF16))
    return parts


def pieces_of(refs, strip_at=0):
    out = []
    for level in range(LEVELS):
        strip_start = strip_at + level * STRIP
        spans = [slice(level * WIDE, (level + 1) * WIDE)] * 2 + [slice(strip_start, strip_start + STRIP)] * 2
        out.append(jnp.concatenate([ref[span] for ref, span in zip(refs, spans)], axis=0))
    return out


def put_pieces(parts, refs):
    for level, part in enumerate(parts):
        at = 0
        for ref, size in zip(refs, (WIDE, WIDE, STRIP, STRIP)):
            ref[level * size : (level + 1) * size] = part[at : at + size]
            at += size


def layer_norm(values):
    centred = values - jnp.mean(values, axis=-1, keepdims=True)
    inverse = lax.rsqrt(jnp.mean(centred * centred, axis=-1, keepdims=True) + EPSILON)
    return centred * inverse, inverse


def stacked(part, scale):
    lane = lax.broadcasted_iota(jnp.int32, (1, QUAD), 1) // HEAD_DIM
    wide = [part * jnp.where(lane == h, scale, 0.0).astype(BF16) for h in range(4)]
    return jnp.concatenate(wide, axis=0)


def unstacked(product):
    lane = lax.broadcasted_iota(jnp.int32, (WINDOW, QUAD), 1) // HEAD_DIM
    out = product[:WINDOW]
    for h in range(1, 4):
        out = jnp.where(lane == h, product[h * WINDOW : (h + 1) * WINDOW], out)
    return out


def soft(keys_stacked, queries, bias):
    out = []
    for h in range(4):
        scores = dot_nt(keys_stacked[h * WINDOW : (h + 1) * WINDOW], queries)
        if bias is not None:
            scores = scores + bias
        raised = jnp.exp(scores - jnp.max(scores, axis=0, keepdims=True))
        out.append(raised * (1.0 / jnp.sum(raised, axis=0, keepdims=True)))
    return out


def places(w, quad):
    span = slice(w * WINDOW, (w + 1) * WINDOW)
    return span, [slice(n * D + quad * QUAD, n * D + (quad + 1) * QUAD) for n in range(3)]


def forward_kernel(
    tokens, cotangent, w_qkv, w_proj, plain, cut, strips,
    keep, tall, side, corner, values_out, normed_out, packed, probs_out, mixed,
):
    values = gathered(plain, [tokens[:LEVEL], tokens[LEVEL:]])
    values_out[...] = values.astype(BF16)
    values_out.flush()
    normed = layer_norm(values)[0].astype(BF16)
    normed_out[...] = normed
    normed_out.flush()
    packed[...] = dot(normed, w_qkv[...]).astype(BF16)
    packed.flush()
    for w in range(WINDOWS):
        for quad in range(2):
            span, at = places(w, quad)
            queries, keys, vals = [packed[span, at[n]] for n in range(3)]
            probs = jnp.concatenate(soft(stacked(keys, SCALE), queries, None), axis=0).astype(BF16)
            probs_out[2 * w + quad] = probs
            mixed[span, at[0]] = dot_tn(probs, stacked(vals, 1.0)).astype(BF16)
    probs_out.flush()
    mixed.flush()
    first = values + dot(mixed[...], w_proj[...])
    put_pieces(scattered(cut, first), (keep, tall, side, corner))
    for level in range(LEVELS):
        part = dot(strips[...], cotangent[level * LEVEL : (level + 1) * LEVEL]).astype(BF16)
        at = slice((LEVELS + level) * STRIP, (LEVELS + level + 1) * STRIP)
        side[at] = part[:STRIP]
        corner[at] = part[STRIP:]


def attention_backward(packed, probs, probs_low, d_mixed, d_packed, span, at, keys_stacked, vals_stacked):
    d_scores = []
    for h in range(4):
        d_probs = dot_nt(vals_stacked[h * WINDOW : (h + 1) * WINDOW], d_mixed)
        inner = jnp.sum(probs[h] * d_probs, axis=0, keepdims=True)
        d_scores.append((probs[h] * (d_probs - inner)).astype(BF16))
    d_scores = jnp.concatenate(d_scores, axis=0)
    d_packed[span, at[0]] = dot_tn(d_scores, keys_stacked).astype(BF16)
    d_packed[span, at[1]] = (unstacked(dot(d_scores, packed[span, at[0]])) * SCALE).astype(BF16)
    d_packed[span, at[2]] = unstacked(dot(probs_low, d_mixed)).astype(BF16)


def input_gradient(values, gradient, d_packed, w_qkv):
    standard, inverse = layer_norm(values)
    d_normed = dot_nt(d_packed, w_qkv)
    d_input = inverse * (
        d_normed
        - jnp.mean(d_normed, axis=-1, keepdims=True)
        - standard * jnp.mean(d_normed * standard, axis=-1, keepdims=True)
    )
    return gradient.astype(F32) + d_input


def weight_gradients(core, normed, d_packed, mixed, gradient, grads, kept, sent):
    grads[:, :48] = dot_tn(d_packed, normed).astype(BF16).reshape(32, 48, D)
    grads[:, 48:] = dot_tn(gradient, mixed).astype(BF16).reshape(32, 16, D)
    for j in range(16):
        kept[j] = grads[2 * j + core[0]]
        sent[j] = grads[2 * j + 1 - core[0]]


def shifted_kernel(
    core, keep, tall, side, corner, cotangent, tall_g, w_qkv, w_proj, gather, gather_g, scatter, bias,
    keep_out, tall_out, side_out, corner_out, kept, sent,
    packed, d_mixed_all, mixed, d_packed, grads,
):
    sources = []
    for level in range(LEVELS):
        own = cotangent[level * LEVEL + LEVEL // 2 : (level + 1) * LEVEL]
        beside = [ref[(LEVELS + level) * STRIP : (LEVELS + level + 1) * STRIP] for ref in (side, corner)]
        sources.append(
            jnp.concatenate([own, tall_g[level * (LEVEL // 2) : (level + 1) * (LEVEL // 2)], *beside], axis=0)
        )
    gradient = gathered(gather_g, sources).astype(BF16)
    d_mixed_all[...] = dot_nt(gradient, w_proj[...]).astype(BF16)
    values = gathered(gather, pieces_of((keep, tall, side, corner)))
    normed = layer_norm(values)[0].astype(BF16)
    packed[...] = dot(normed, w_qkv[...]).astype(BF16)
    for w in range(WINDOWS):
        for quad in range(2):
            span, at = places(w, quad)
            queries, keys, vals = [packed[span, at[n]] for n in range(3)]
            keys_stacked, vals_stacked = stacked(keys, SCALE), stacked(vals, 1.0)
            probs = soft(keys_stacked, queries, bias[...])
            probs_low = jnp.concatenate(probs, axis=0).astype(BF16)
            mixed[span, at[0]] = dot_tn(probs_low, vals_stacked).astype(BF16)
            attention_backward(
                packed, probs, probs_low, d_mixed_all[span, at[0]], d_packed, span, at, keys_stacked, vals_stacked
            )
    weight_gradients(core, normed, d_packed[...], mixed[...], gradient, grads, kept, sent)
    kept.flush()
    sent.flush()
    result = input_gradient(values, gradient, d_packed[...], w_qkv[...])
    put_pieces(scattered(scatter, result), (keep_out, tall_out, side_out, corner_out))


def plain_kernel(
    core, keep, tall, side, corner, w_proj, join, packed, probs_in, mixed, normed,
    gradient_out, d_packed, kept, sent,
    d_mixed_all, grads,
):
    gradient = gathered(join, pieces_of((keep, tall, side, corner))).astype(BF16)
    gradient_out[...] = gradient
    gradient_out.flush()
    d_mixed_all[...] = dot_nt(gradient, w_proj[...]).astype(BF16)
    for w in range(WINDOWS):
        for quad in range(2):
            span, at = places(w, quad)
            keys_stacked, vals_stacked = stacked(packed[span, at[1]], SCALE), stacked(packed[span, at[2]], 1.0)
            probs_low = probs_in[2 * w + quad]
            probs = [probs_low[h * WINDOW : (h + 1) * WINDOW].astype(F32) for h in range(4)]
            attention_backward(
                packed, probs, probs_low, d_mixed_all[span, at[0]], d_packed, span, at, keys_stacked, vals_stacked
            )
    d_packed.flush()
    weight_gradients(core, normed[...], d_packed[...], mixed[...], gradient, grads, kept, sent)
    kept.flush()
    sent.flush()


def finish_kernel(values, gradient, d_packed, w_qkv, unplain, d_tokens):
    result = input_gradient(values[...].astype(F32), gradient[...], d_packed[...], w_qkv[...])
    for level, part in enumerate(scattered(unplain, result)):
        d_tokens[level * LEVEL : (level + 1) * LEVEL] = part


def swapped_halves(top, bottom):
    left = lax.broadcasted_iota(jnp.int32, top.shape, 1) < top.shape[1] // 2
    turned = [pltpu.roll(x, top.shape[1] // 2, 1) for x in (top, bottom)]
    return jnp.where(left, top, turned[1]), jnp.where(left, turned[0], bottom)


def core_sums(kept, received, landing, sems):
    half = kept.shape[0] // 2
    spans = [slice(pair * 128, (pair + 1) * 128) for pair in range(4)]
    copies = [pltpu.make_async_copy(kept.at[:, at], landing.at[n], sems.at[n]) for n, at in enumerate(spans)]
    for copy in copies:
        copy.start()
    for pair, at in enumerate(spans):
        copies[pair].wait()
        total = landing[pair].astype(F32) + received[:, at].astype(F32)
        for odd, part in enumerate(swapped_halves(total[:half], total[half:])):
            yield 2 * pair + odd, part.astype(BF16)


def core_sum_kernel(kept, received, out, landing, made, sems):
    leaving = []
    for lat, part in core_sums(kept, received, landing, sems):
        made[lat] = part
        leaving.append(pltpu.make_async_copy(made.at[lat], out.at[lat], sems.at[4 + lat]))
        leaving[-1].start()
    for copy in leaving:
        copy.wait()


def core_cut_kernel(place, kept, received, *refs):
    outs, (landing, held, sems) = refs[:-3], refs[-3:]
    for lat, part in core_sums(kept, received, landing, sems):
        held[lat // 2, lat % 2] = part
    for step, out in enumerate(outs):
        out[...] = held[lax.rem(place[0] + step, 4)]


def far_sum_kernel(place, one, two, three, four, kept, sent):
    total = one[...].astype(F32) + two[...].astype(F32) + three[...].astype(F32) + four[...].astype(F32)
    first = place[0] == 0
    kept[...] = jnp.where(first, total[0], total[1]).astype(BF16)
    sent[...] = jnp.where(first, total[1], total[0]).astype(BF16)


def lat_sum_kernel(parts, kept, received, out):
    total = parts[0].astype(F32)
    for a in range(1, 8):
        total = total + parts[a].astype(F32)
    other = kept[...].astype(F32) + received[...].astype(F32)
    for block, held in enumerate((total, other)):
        for j in range(8):
            low, high = swapped_halves(held[64 * j : 64 * j + 32], held[64 * j + 32 : 64 * j + 64])
            out[j, block] = low.astype(BF16)
            out[j + 8, block] = high.astype(BF16)


def lon_sum_kernel(parts, grad_qkv, grad_proj):
    for block in range(2):
        total = parts[0, block].astype(F32)
        for j in range(1, 16):
            total = total + parts[j, block].astype(F32)
        whole = jnp.concatenate([total, pltpu.roll(total, 64, 1)], axis=0)
        grad_qkv[block] = whole[:48, :64]
        grad_proj[block] = whole[48:, :64]


def shape(*dims, kind=BF16):
    return jax.ShapeDtypeStruct(dims, kind)


def call(kernel, name, outs, *operands, scratch=(), scalar=False, fetch=None, store=(), apart=(), own_out=False, limit=SMALL, micros=1):
    fetch = fetch or {}
    several = outs if isinstance(outs, tuple) else (outs,)
    cut = np.cumsum([0, len(operands), len(several), len(scratch), len(fetch), len(store)])

    def body(*refs):
        ins, results, own, landing, leaving = [list(refs[a:b]) for a, b in zip(cut[:-1], cut[1:])]
        for at, (n, index) in enumerate(fetch.items()):
            ins[n] = Fetched(ins[n] if index is None else ins[n].at[index], landing[at], refs[-2].at[at])
        for at, n in enumerate(store):
            results[n] = Stored(leaving[at], results[n], refs[-1].at[at])
        kernel(*ins, *results, *own)
        for n in store:
            results[n].copy.wait()

    held = [pltpu.VMEM(dims, BF16) if isinstance(dims, tuple) else dims for dims in scratch]
    for n, index in fetch.items():
        held.append(pltpu.VMEM(operands[n].shape if index is None else operands[n].shape[1:], BF16))
    held += [pltpu.VMEM(several[n].shape, BF16) for n in store]
    if fetch or store:
        held += [pltpu.SemaphoreType.DMA((max(1, len(group)),)) for group in (fetch, store)]
    kinds = [pltpu.HBM if n in fetch or n in apart else pltpu.VMEM for n in range(len(operands))]
    if scalar:
        kinds[0] = pltpu.SMEM
    specs = tuple(pl.BlockSpec(memory_space=pltpu.HBM if own_out or n in store else pltpu.VMEM) for n in range(len(several)))
    return pl.pallas_call(
        body,
        out_shape=outs,
        in_specs=[pl.BlockSpec(memory_space=kind) for kind in kinds],
        out_specs=specs if isinstance(outs, tuple) else specs[0],
        scratch_shapes=held,
        compiler_params=pltpu.CompilerParams(vmem_limit_bytes=limit * 1024 * 1024),
        cost_estimate=pl.CostEstimate(
            flops=micros * PEAK_FLOPS, bytes_accessed=micros * PEAK_BYTES, transcendentals=0
        ),
        name=name,
    )(*operands)


def moved(piece, lat, lon):
    n_lat, n_lon = lax.axis_size("lat"), lax.axis_size("lon")
    if lon == 0:
        return lax.ppermute(piece, "lat", [(i, (i + lat) % n_lat) for i in range(n_lat)])
    if lat == 0:
        return lax.ppermute(piece, "lon", [(i, (i + lon) % n_lon) for i in range(n_lon)])
    route = [
        (a * n_lon + b, (a + lat) % n_lat * n_lon + (b + lon) % n_lon)
        for a in range(n_lat)
        for b in range(n_lon)
    ]
    return lax.ppermute(piece, ("lat", "lon"), route)


def exchanged(tall, side, corner, step):
    corner = moved(corner, step, step)
    side = moved(side, 0, step)
    return moved(tall, step, 0), side, corner


def core_swapped(sent):
    return lax.ppermute(sent, "lon", [(i, i ^ 1) for i in range(lax.axis_size("lon"))]).reshape(1024, D)


def core_reduced(kept, sent):
    return call(
        core_sum_kernel, "core_sum", shape(8, 512, 128), kept.reshape(1024, D), core_swapped(sent),
        scratch=[(4, 1024, 128), (8, 512, 128), pltpu.SemaphoreType.DMA((12,))], apart=(0,), own_out=True, limit=12,
    )


def core_cut(kept, sent):
    place = (lax.axis_index("lat") // 2).astype(jnp.int32).reshape(1)
    return call(
        core_cut_kernel, "core_cut", (shape(2, 512, 128),) * 4, place, kept.reshape(1024, D), core_swapped(sent),
        scratch=[(4, 1024, 128), (4, 2, 512, 128), pltpu.SemaphoreType.DMA((4,))], scalar=True, apart=(1,), limit=12,
    )


def far_reduced(parts):
    n = lax.axis_size("lat")
    arrived = [parts[0]]
    for step in (2, 3, 1):
        arrived.append(lax.ppermute(parts[step], "lat", [(i, (i + 2 * step) % n) for i in range(n)]))
    place = (lax.axis_index("lat") % 2).astype(jnp.int32).reshape(1)
    kept, sent = call(far_sum_kernel, "far_sum", (shape(512, 128),) * 2, place, *arrived, scalar=True)
    return kept, sent


def reduced(chunks_one, parts_two):
    kept, sent = parts_two
    received = lax.ppermute(sent, "lat", [(i, i ^ 1) for i in range(lax.axis_size("lat"))])
    arrived = lax.all_to_all(chunks_one, "lat", 0, 0, tiled=True)
    both = call(lat_sum_kernel, "lat_sum", shape(16, 2, 32, 128), arrived, kept, received)
    groups = [[2 * j + core for j in range(16)] for core in range(2)]
    arrived = lax.all_to_all(both, "lon", 0, 0, tiled=True, axis_index_groups=groups)
    grads = call(lon_sum_kernel, "lon_sum", (shape(2, 48, 64, kind=F32), shape(2, 16, 64, kind=F32)), arrived)
    return [grad.transpose(0, 2, 1) for grad in grads]


def body(tokens, cotangent, qkv_weights, proj_weights):
    plain, unplain = selection((LEVEL, LEVEL), PLAIN), selection((LEVEL, LEVEL), flipped(PLAIN))
    join, cut = selection((LEVEL, PIECES), JOIN), selection((PIECES, LEVEL), flipped(JOIN))
    shift, unshift = selection((LEVEL, PIECES), SHIFT), selection((PIECES, LEVEL), flipped(SHIFT))
    shift_half, strips = selection((LEVEL, LEVEL + 2 * STRIP), SHIFT_HALF), selection((2 * STRIP, LEVEL), STRIPS)
    core = (lax.axis_index("lon") % 2).astype(jnp.int32).reshape(1)
    last_lat = lax.axis_index("lat") == lax.axis_size("lat") - 1
    label = (np.arange(WINDOW) // WIN_LON % WIN_LAT >= HALF_LAT).astype(np.int32)
    bias = jnp.where(last_lat & (label[:, None] != label[None, :]), MASKED, 0.0).astype(F32)
    field, flat = shape(TOKENS, D), tokens.reshape(TOKENS, D)
    wide, strip, pair = [shape(LEVELS * rows, D) for rows in (WIDE, STRIP, 2 * STRIP)]
    packed_field = shape(TOKENS, 3 * D)
    half = shape(16, 64, D)

    tall_g = moved(cotangent[:, :HALF_LAT].reshape(HALF, D), -1, 0)
    flat_g = cotangent.reshape(TOKENS, D)
    keep, tall, side, corner, values, normed, packed, probs, mixed = call(
        forward_kernel,
        "forward",
        (wide, wide, pair, pair, field, field, packed_field, shape(2 * WINDOWS, 4 * WINDOW, WINDOW), field),
        flat, flat_g, qkv_weights, proj_weights, plain, cut, strips,
        fetch={4: None, 0: None, 2: 0, 3: 0, 5: None, 6: None, 1: None},
        store=(4, 5, 6, 7, 8),
        limit=58,
        micros=9,
    )
    tall, side, corner = exchanged(tall, side, corner, -1)
    keep, tall, side, corner, kept_two, sent_two = call(
        shifted_kernel,
        "backward_shifted",
        (wide, wide, strip, strip, half, half),
        core, keep, tall, side, corner, flat_g, tall_g, qkv_weights, proj_weights, shift, shift_half, unshift, bias,
        scratch=[(TOKENS, 3 * D), (TOKENS, D), (TOKENS, D), (TOKENS, 3 * D), (32, 64, D)],
        scalar=True,
        fetch={5: None, 10: None, 8: 1, 9: None, 7: 1, 11: None},
        store=(4, 5),
        limit=51,
        micros=18,
    )
    tall, side, corner = exchanged(tall, side, corner, 1)
    parts_two = far_reduced(core_cut(kept_two, sent_two))
    gradient, d_packed, kept_one, sent_one = call(
        plain_kernel,
        "backward_plain",
        (field, packed_field, half, half),
        core, keep, tall, side, corner, proj_weights, join, packed, probs, mixed, normed,
        scratch=[(TOKENS, D), (32, 64, D)],
        scalar=True,
        fetch={6: None, 5: 0, 7: None, 8: None, 10: None, 9: None},
        store=(0, 1, 2, 3),
        limit=51,
        micros=10,
    )
    d_tokens = call(
        finish_kernel,
        "finish_plain",
        field,
        values, gradient, d_packed, qkv_weights, unplain,
        fetch={2: None, 3: 0, 0: None, 1: None, 4: None},
        limit=LARGE,
        micros=5,
    )
    sent_one, parts_two = lax.optimization_barrier((sent_one, parts_two))
    grad_qkv, grad_proj = reduced(core_reduced(kept_one, sent_one), parts_two)
    return d_tokens.reshape(tokens.shape), grad_qkv, grad_proj


def solution(mesh):
    return jax.shard_map(
        body,
        mesh=mesh,
        in_specs=(P(None, "lat", "lon", None), P(None, "lat", "lon", None), P(), P()),
        out_specs=(P(None, "lat", "lon", None), P(None, "lat", "lon"), P(None, "lat", "lon")),
        check_vma=False,
    )
```

```python
import functools

import jax
import jax.numpy as jnp
import numpy as np
from jax import lax
from jax.experimental import pallas as pl
from jax.experimental.pallas import tpu as pltpu
from jax.sharding import PartitionSpec as P

D = 512
HEADS = 8
HEAD_DIM = 64
LEVELS = 2
WIN_LAT = 12
WIN_LON = 6
HALF_LAT = 6
HALF_LON = 3
ROWS = 12
COLS = 24
TOKENS = LEVELS * ROWS * COLS
WINDOW = LEVELS * WIN_LAT * WIN_LON
WINDOWS = TOKENS // WINDOW
HALF = TOKENS // 2
QUAD = 4 * HEAD_DIM
LEVEL = ROWS * COLS
SEGMENT = WIN_LAT * WIN_LON
WIDE = 128
STRIP = 32
PIECES = 2 * WIDE + 2 * STRIP
EPSILON = 1e-05
MASKED = -1000000000.0
SCALE = HEAD_DIM ** (-0.5)
LARGE = 58
SMALL = 6
PEAK_FLOPS = 1_150_000_000
PEAK_BYTES = 3_690_000
F32 = jnp.float32
BF16 = jnp.bfloat16


def window_order(row, col):
    return (col // WIN_LON) * SEGMENT + row * WIN_LON + col % WIN_LON


def field_order(row, col):
    return row * COLS + col


def piece_order(row, col):
    upper = int(row < HALF_LAT)
    at = row % HALF_LAT
    if col < HALF_LON:
        return 2 * WIDE + STRIP * upper + at * HALF_LON + col
    return WIDE * upper + at * (COLS - HALF_LON) + col - HALF_LON


def half_order(row, col):
    if col >= COLS:
        return LEVEL + piece_order(row, col - COLS) - 2 * WIDE
    return LEVEL // 2 * int(row < HALF_LAT) + (row % HALF_LAT) * COLS + col


def selection(shape, pairs):
    out = np.zeros(shape, np.float32)
    for row, column in pairs:
        out[row, column] = 1
    return jnp.asarray(out, BF16)


CELLS = list(np.ndindex(ROWS, COLS))
PLAIN = [(window_order(*cell), field_order(*cell)) for cell in CELLS]
JOIN = [(window_order(*cell), piece_order(*cell)) for cell in CELLS]
STRIPS = [(piece_order(*cell) - 2 * WIDE, field_order(*cell)) for cell in CELLS if cell[1] < HALF_LON]
SHIFTED = [((r + HALF_LAT) % ROWS, c + HALF_LON) for r, c in CELLS]
SHIFT = [(window_order(*cell), piece_order(r, c % COLS)) for cell, (r, c) in zip(CELLS, SHIFTED)]
SHIFT_HALF = [(window_order(*cell), half_order(r, c)) for cell, (r, c) in zip(CELLS, SHIFTED)]


def flipped(pairs):
    return [(column, row) for row, column in pairs]


class Fetched:
    def __init__(self, source, target, sem):
        self.copy, self.target, self.waiting = pltpu.make_async_copy(source, target, sem), target, True
        self.copy.start()

    def __getitem__(self, index):
        if self.waiting:
            self.copy.wait()
            self.waiting = False
        return self.target[index]


class Stored:
    def __init__(self, source, target, sem):
        self.copy, self.source = pltpu.make_async_copy(source, target, sem), source

    def __getitem__(self, index):
        return self.source[index]

    def __setitem__(self, index, value):
        self.source[index] = value

    def flush(self):
        self.copy.start()


def dot(a, b):
    return lax.dot_general(a, b, (((1,), (0,)), ((), ())), preferred_element_type=F32)


def dot_nt(a, b):
    return lax.dot_general(a, b, (((1,), (1,)), ((), ())), preferred_element_type=F32)


def dot_tn(a, b):
    return lax.dot_general(a, b, (((0,), (0,)), ((), ())), preferred_element_type=F32)


def gathered(matrix, levels):
    parts = [dot(matrix[...], level) for level in levels]
    segments = [part[w * SEGMENT : (w + 1) * SEGMENT] for w in range(WINDOWS) for part in parts]
    return jnp.concatenate(segments, axis=0)


def scattered(matrix, values):
    parts = []
    for level in range(LEVELS):
        starts = [w * WINDOW + level * SEGMENT for w in range(WINDOWS)]
        own = jnp.concatenate([values[start : start + SEGMENT] for start in starts], axis=0)
        parts.append(dot(matrix[...], own.astype(BF16)).astype(BF16))
    return parts


def pieces_of(refs, strip_at=0):
    out = []
    for level in range(LEVELS):
        strip_start = strip_at + level * STRIP
        spans = [slice(level * WIDE, (level + 1) * WIDE)] * 2 + [slice(strip_start, strip_start + STRIP)] * 2
        out.append(jnp.concatenate([ref[span] for ref, span in zip(refs, spans)], axis=0))
    return out


def put_pieces(parts, refs):
    for level, part in enumerate(parts):
        at = 0
        for ref, size in zip(refs, (WIDE, WIDE, STRIP, STRIP)):
            ref[level * size : (level + 1) * size] = part[at : at + size]
            at += size


def layer_norm(values):
    centred = values - jnp.mean(values, axis=-1, keepdims=True)
    inverse = lax.rsqrt(jnp.mean(centred * centred, axis=-1, keepdims=True) + EPSILON)
    return centred * inverse, inverse


def stacked(part, scale):
    lane = lax.broadcasted_iota(jnp.int32, (1, QUAD), 1) // HEAD_DIM
    wide = [part * jnp.where(lane == h, scale, 0.0).astype(BF16) for h in range(4)]
    return jnp.concatenate(wide, axis=0)


def unstacked(product):
    lane = lax.broadcasted_iota(jnp.int32, (WINDOW, QUAD), 1) // HEAD_DIM
    out = product[:WINDOW]
    for h in range(1, 4):
        out = jnp.where(lane == h, product[h * WINDOW : (h + 1) * WINDOW], out)
    return out


def soft(keys_stacked, queries, bias):
    out = []
    for h in range(4):
        scores = dot_nt(keys_stacked[h * WINDOW : (h + 1) * WINDOW], queries)
        if bias is not None:
            scores = scores + bias
        raised = jnp.exp(scores - jnp.max(scores, axis=0, keepdims=True))
        out.append(raised * (1.0 / jnp.sum(raised, axis=0, keepdims=True)))
    return out


def places(w, quad):
    span = slice(w * WINDOW, (w + 1) * WINDOW)
    return span, [slice(n * D + quad * QUAD, n * D + (quad + 1) * QUAD) for n in range(3)]


def forward_kernel(
    tokens, cotangent, w_qkv, w_proj, plain, cut, strips,
    keep, tall, side, corner, values_out, normed_out, packed, probs_out, mixed,
):
    values = gathered(plain, [tokens[:LEVEL], tokens[LEVEL:]])
    values_out[...] = values.astype(BF16)
    values_out.flush()
    normed = layer_norm(values)[0].astype(BF16)
    normed_out[...] = normed
    normed_out.flush()
    packed[...] = dot(normed, w_qkv[...]).astype(BF16)
    packed.flush()
    for w in range(WINDOWS):
        for quad in range(2):
            span, at = places(w, quad)
            queries, keys, vals = [packed[span, at[n]] for n in range(3)]
            probs = jnp.concatenate(soft(stacked(keys, SCALE), queries, None), axis=0).astype(BF16)
            probs_out[2 * w + quad] = probs
            mixed[span, at[0]] = dot_tn(probs, stacked(vals, 1.0)).astype(BF16)
    probs_out.flush()
    mixed.flush()
    first = values + dot(mixed[...], w_proj[...])
    put_pieces(scattered(cut, first), (keep, tall, side, corner))
    for level in range(LEVELS):
        part = dot(strips[...], cotangent[level * LEVEL : (level + 1) * LEVEL]).astype(BF16)
        at = slice((LEVELS + level) * STRIP, (LEVELS + level + 1) * STRIP)
        side[at] = part[:STRIP]
        corner[at] = part[STRIP:]


def attention_backward(packed, probs, probs_low, d_mixed, d_packed, span, at, keys_stacked, vals_stacked):
    d_scores = []
    for h in range(4):
        d_probs = dot_nt(vals_stacked[h * WINDOW : (h + 1) * WINDOW], d_mixed)
        inner = jnp.sum(probs[h] * d_probs, axis=0, keepdims=True)
        d_scores.append((probs[h] * (d_probs - inner)).astype(BF16))
    d_scores = jnp.concatenate(d_scores, axis=0)
    d_packed[span, at[0]] = dot_tn(d_scores, keys_stacked).astype(BF16)
    d_packed[span, at[1]] = (unstacked(dot(d_scores, packed[span, at[0]])) * SCALE).astype(BF16)
    d_packed[span, at[2]] = unstacked(dot(probs_low, d_mixed)).astype(BF16)


def input_gradient(values, gradient, d_packed, w_qkv):
    standard, inverse = layer_norm(values)
    d_normed = dot_nt(d_packed, w_qkv)
    d_input = inverse * (
        d_normed
        - jnp.mean(d_normed, axis=-1, keepdims=True)
        - standard * jnp.mean(d_normed * standard, axis=-1, keepdims=True)
    )
    return gradient.astype(F32) + d_input


def weight_gradients(core, normed, d_packed, mixed, gradient, grads, kept, sent):
    grads[:, :48] = dot_tn(d_packed, normed).astype(BF16).reshape(32, 48, D)
    grads[:, 48:] = dot_tn(gradient, mixed).astype(BF16).reshape(32, 16, D)
    for j in range(16):
        kept[j] = grads[2 * j + core[0]]
        sent[j] = grads[2 * j + 1 - core[0]]


def shifted_kernel(
    core, keep, tall, side, corner, cotangent, tall_g, w_qkv, w_proj, gather, gather_g, scatter, bias,
    keep_out, tall_out, side_out, corner_out, kept, sent,
    packed, d_mixed_all, mixed, d_packed, grads,
):
    sources = []
    for level in range(LEVELS):
        own = cotangent[level * LEVEL + LEVEL // 2 : (level + 1) * LEVEL]
        beside = [ref[(LEVELS + level) * STRIP : (LEVELS + level + 1) * STRIP] for ref in (side, corner)]
        sources.append(
            jnp.concatenate([own, tall_g[level * (LEVEL // 2) : (level + 1) * (LEVEL // 2)], *beside], axis=0)
        )
    gradient = gathered(gather_g, sources).astype(BF16)
    d_mixed_all[...] = dot_nt(gradient, w_proj[...]).astype(BF16)
    values = gathered(gather, pieces_of((keep, tall, side, corner)))
    normed = layer_norm(values)[0].astype(BF16)
    packed[...] = dot(normed, w_qkv[...]).astype(BF16)
    for w in range(WINDOWS):
        for quad in range(2):
            span, at = places(w, quad)
            queries, keys, vals = [packed[span, at[n]] for n in range(3)]
            keys_stacked, vals_stacked = stacked(keys, SCALE), stacked(vals, 1.0)
            probs = soft(keys_stacked, queries, bias[...])
            probs_low = jnp.concatenate(probs, axis=0).astype(BF16)
            mixed[span, at[0]] = dot_tn(probs_low, vals_stacked).astype(BF16)
            attention_backward(
                packed, probs, probs_low, d_mixed_all[span, at[0]], d_packed, span, at, keys_stacked, vals_stacked
            )
    weight_gradients(core, normed, d_packed[...], mixed[...], gradient, grads, kept, sent)
    kept.flush()
    sent.flush()
    result = input_gradient(values, gradient, d_packed[...], w_qkv[...])
    put_pieces(scattered(scatter, result), (keep_out, tall_out, side_out, corner_out))


def plain_kernel(
    core, keep, tall, side, corner, w_proj, join, packed, probs_in, mixed, normed,
    gradient_out, d_packed, kept, sent,
    d_mixed_all, grads,
):
    gradient = gathered(join, pieces_of((keep, tall, side, corner))).astype(BF16)
    gradient_out[...] = gradient
    gradient_out.flush()
    d_mixed_all[...] = dot_nt(gradient, w_proj[...]).astype(BF16)
    for w in range(WINDOWS):
        for quad in range(2):
            span, at = places(w, quad)
            keys_stacked, vals_stacked = stacked(packed[span, at[1]], SCALE), stacked(packed[span, at[2]], 1.0)
            probs_low = probs_in[2 * w + quad]
            probs = [probs_low[h * WINDOW : (h + 1) * WINDOW].astype(F32) for h in range(4)]
            attention_backward(
                packed, probs, probs_low, d_mixed_all[span, at[0]], d_packed, span, at, keys_stacked, vals_stacked
            )
    d_packed.flush()
    weight_gradients(core, normed[...], d_packed[...], mixed[...], gradient, grads, kept, sent)
    kept.flush()
    sent.flush()


def finish_kernel(values, gradient, d_packed, w_qkv, unplain, d_tokens):
    result = input_gradient(values[...].astype(F32), gradient[...], d_packed[...], w_qkv[...])
    for level, part in enumerate(scattered(unplain, result)):
        d_tokens[level * LEVEL : (level + 1) * LEVEL] = part


def swapped_halves(top, bottom):
    left = lax.broadcasted_iota(jnp.int32, top.shape, 1) < top.shape[1] // 2
    turned = [pltpu.roll(x, top.shape[1] // 2, 1) for x in (top, bottom)]
    return jnp.where(left, top, turned[1]), jnp.where(left, turned[0], bottom)


def core_sums(kept, received, landing, sems):
    half = kept.shape[0] // 2
    spans = [slice(pair * 128, (pair + 1) * 128) for pair in range(4)]
    copies = [pltpu.make_async_copy(kept.at[:, at], landing.at[n], sems.at[n]) for n, at in enumerate(spans)]
    for copy in copies:
        copy.start()
    for pair, at in enumerate(spans):
        copies[pair].wait()
        total = landing[pair].astype(F32) + received[:, at].astype(F32)
        for odd, part in enumerate(swapped_halves(total[:half], total[half:])):
            yield 2 * pair + odd, part.astype(BF16)


def core_sum_kernel(kept, received, out, landing, made, sems):
    leaving = []
    for lat, part in core_sums(kept, received, landing, sems):
        made[lat] = part
        leaving.append(pltpu.make_async_copy(made.at[lat], out.at[lat], sems.at[4 + lat]))
        leaving[-1].start()
    for copy in leaving:
        copy.wait()


def core_cut_kernel(place, kept, received, *refs):
    outs, (landing, held, sems) = refs[:-3], refs[-3:]
    for lat, part in core_sums(kept, received, landing, sems):
        held[lat // 2, lat % 2] = part
    for step, out in enumerate(outs):
        out[...] = held[lax.rem(place[0] + step, 4)]


def far_sum_kernel(place, one, two, three, four, kept, sent):
    total = one[...].astype(F32) + two[...].astype(F32) + three[...].astype(F32) + four[...].astype(F32)
    first = place[0] == 0
    kept[...] = jnp.where(first, total[0], total[1]).astype(BF16)
    sent[...] = jnp.where(first, total[1], total[0]).astype(BF16)


def lat_sum_kernel(parts, kept, received, out):
    total = parts[0].astype(F32)
    for a in range(1, 8):
        total = total + parts[a].astype(F32)
    other = kept[...].astype(F32) + received[...].astype(F32)
    for block, held in enumerate((total, other)):
        for j in range(8):
            low, high = swapped_halves(held[64 * j : 64 * j + 32], held[64 * j + 32 : 64 * j + 64])
            out[j, block] = low.astype(BF16)
            out[j + 8, block] = high.astype(BF16)


def lon_sum_kernel(parts, grad_qkv, grad_proj):
    for block in range(2):
        total = parts[0, block].astype(F32)
        for j in range(1, 16):
            total = total + parts[j, block].astype(F32)
        whole = jnp.concatenate([total, pltpu.roll(total, 64, 1)], axis=0)
        grad_qkv[block] = whole[:48, :64]
        grad_proj[block] = whole[48:, :64]


def shape(*dims, kind=BF16):
    return jax.ShapeDtypeStruct(dims, kind)


def call(kernel, name, outs, *operands, scratch=(), scalar=False, fetch=None, store=(), apart=(), own_out=False, limit=SMALL, micros=1):
    fetch = fetch or {}
    several = outs if isinstance(outs, tuple) else (outs,)
    cut = np.cumsum([0, len(operands), len(several), len(scratch), len(fetch), len(store)])

    def body(*refs):
        ins, results, own, landing, leaving = [list(refs[a:b]) for a, b in zip(cut[:-1], cut[1:])]
        for at, (n, index) in enumerate(fetch.items()):
            ins[n] = Fetched(ins[n] if index is None else ins[n].at[index], landing[at], refs[-2].at[at])
        for at, n in enumerate(store):
            results[n] = Stored(leaving[at], results[n], refs[-1].at[at])
        kernel(*ins, *results, *own)
        for n in store:
            results[n].copy.wait()

    held = [pltpu.VMEM(dims, BF16) if isinstance(dims, tuple) else dims for dims in scratch]
    for n, index in fetch.items():
        held.append(pltpu.VMEM(operands[n].shape if index is None else operands[n].shape[1:], BF16))
    held += [pltpu.VMEM(several[n].shape, BF16) for n in store]
    if fetch or store:
        held += [pltpu.SemaphoreType.DMA((max(1, len(group)),)) for group in (fetch, store)]
    kinds = [pltpu.HBM if n in fetch or n in apart else pltpu.VMEM for n in range(len(operands))]
    if scalar:
        kinds[0] = pltpu.SMEM
    specs = tuple(pl.BlockSpec(memory_space=pltpu.HBM if own_out or n in store else pltpu.VMEM) for n in range(len(several)))
    return pl.pallas_call(
        body,
        out_shape=outs,
        in_specs=[pl.BlockSpec(memory_space=kind) for kind in kinds],
        out_specs=specs if isinstance(outs, tuple) else specs[0],
        scratch_shapes=held,
        compiler_params=pltpu.CompilerParams(vmem_limit_bytes=limit * 1024 * 1024),
        cost_estimate=pl.CostEstimate(
            flops=micros * PEAK_FLOPS, bytes_accessed=micros * PEAK_BYTES, transcendentals=0
        ),
        name=name,
    )(*operands)


def moved(piece, lat, lon):
    n_lat, n_lon = lax.axis_size("lat"), lax.axis_size("lon")
    if lon == 0:
        return lax.ppermute(piece, "lat", [(i, (i + lat) % n_lat) for i in range(n_lat)])
    if lat == 0:
        return lax.ppermute(piece, "lon", [(i, (i + lon) % n_lon) for i in range(n_lon)])
    route = [
        (a * n_lon + b, (a + lat) % n_lat * n_lon + (b + lon) % n_lon)
        for a in range(n_lat)
        for b in range(n_lon)
    ]
    return lax.ppermute(piece, ("lat", "lon"), route)


def exchanged(tall, side, corner, step):
    corner = moved(corner, step, step)
    side = moved(side, 0, step)
    return moved(tall, step, 0), side, corner


def core_swapped(sent):
    return lax.ppermute(sent, "lon", [(i, i ^ 1) for i in range(lax.axis_size("lon"))]).reshape(1024, D)


def core_reduced(kept, sent):
    return call(
        core_sum_kernel, "core_sum", shape(8, 512, 128), kept.reshape(1024, D), core_swapped(sent),
        scratch=[(4, 1024, 128), (8, 512, 128), pltpu.SemaphoreType.DMA((12,))], apart=(0,), own_out=True, limit=12,
    )


def core_cut(kept, sent):
    place = (lax.axis_index("lat") // 2).astype(jnp.int32).reshape(1)
    return call(
        core_cut_kernel, "core_cut", (shape(2, 512, 128),) * 4, place, kept.reshape(1024, D), core_swapped(sent),
        scratch=[(4, 1024, 128), (4, 2, 512, 128), pltpu.SemaphoreType.DMA((4,))], scalar=True, apart=(1,), limit=12,
    )


def far_reduced(parts):
    n = lax.axis_size("lat")
    arrived = [parts[0]]
    for step in (2, 3, 1):
        arrived.append(lax.ppermute(parts[step], "lat", [(i, (i + 2 * step) % n) for i in range(n)]))
    place = (lax.axis_index("lat") % 2).astype(jnp.int32).reshape(1)
    kept, sent = call(far_sum_kernel, "far_sum", (shape(512, 128),) * 2, place, *arrived, scalar=True)
    return kept, sent


def reduced(chunks_one, parts_two, d_tokens):
    kept, sent = parts_two
    received = lax.ppermute(sent, "lat", [(i, i ^ 1) for i in range(lax.axis_size("lat"))])
    chunks_one, received = lax.optimization_barrier((chunks_one, received))
    arrived = lax.all_to_all(chunks_one, "lat", 0, 0, tiled=True)
    arrived, d_tokens = lax.optimization_barrier((arrived, d_tokens))
    both = call(lat_sum_kernel, "lat_sum", shape(16, 2, 32, 128), arrived, kept, received)
    groups = [[2 * j + core for j in range(16)] for core in range(2)]
    arrived = lax.all_to_all(both, "lon", 0, 0, tiled=True, axis_index_groups=groups)
    grads = call(lon_sum_kernel, "lon_sum", (shape(2, 48, 64, kind=F32), shape(2, 16, 64, kind=F32)), arrived)
    return d_tokens, *[grad.transpose(0, 2, 1) for grad in grads]


def body(tokens, cotangent, qkv_weights, proj_weights):
    plain, unplain = selection((LEVEL, LEVEL), PLAIN), selection((LEVEL, LEVEL), flipped(PLAIN))
    join, cut = selection((LEVEL, PIECES), JOIN), selection((PIECES, LEVEL), flipped(JOIN))
    shift, unshift = selection((LEVEL, PIECES), SHIFT), selection((PIECES, LEVEL), flipped(SHIFT))
    shift_half, strips = selection((LEVEL, LEVEL + 2 * STRIP), SHIFT_HALF), selection((2 * STRIP, LEVEL), STRIPS)
    core = (lax.axis_index("lon") % 2).astype(jnp.int32).reshape(1)
    last_lat = lax.axis_index("lat") == lax.axis_size("lat") - 1
    label = (np.arange(WINDOW) // WIN_LON % WIN_LAT >= HALF_LAT).astype(np.int32)
    bias = jnp.where(last_lat & (label[:, None] != label[None, :]), MASKED, 0.0).astype(F32)
    field, flat = shape(TOKENS, D), tokens.reshape(TOKENS, D)
    wide, strip, pair = [shape(LEVELS * rows, D) for rows in (WIDE, STRIP, 2 * STRIP)]
    packed_field = shape(TOKENS, 3 * D)
    half = shape(16, 64, D)

    tall_g = moved(cotangent[:, :HALF_LAT].reshape(HALF, D), -1, 0)
    flat_g = cotangent.reshape(TOKENS, D)
    keep, tall, side, corner, values, normed, packed, probs, mixed = call(
        forward_kernel,
        "forward",
        (wide, wide, pair, pair, field, field, packed_field, shape(2 * WINDOWS, 4 * WINDOW, WINDOW), field),
        flat, flat_g, qkv_weights, proj_weights, plain, cut, strips,
        fetch={4: None, 0: None, 2: 0, 3: 0, 5: None, 6: None, 1: None},
        store=(4, 5, 6, 7, 8),
        limit=58,
        micros=9,
    )
    tall, side, corner = exchanged(tall, side, corner, -1)
    keep, tall, side, corner, kept_two, sent_two = call(
        shifted_kernel,
        "backward_shifted",
        (wide, wide, strip, strip, half, half),
        core, keep, tall, side, corner, flat_g, tall_g, qkv_weights, proj_weights, shift, shift_half, unshift, bias,
        scratch=[(TOKENS, 3 * D), (TOKENS, D), (TOKENS, D), (TOKENS, 3 * D), (32, 64, D)],
        scalar=True,
        fetch={5: None, 10: None, 8: 1, 9: None, 7: 1, 11: None},
        store=(4, 5),
        limit=51,
        micros=18,
    )
    tall, side, corner = exchanged(tall, side, corner, 1)
    parts_two = far_reduced(core_cut(kept_two, sent_two))
    gradient, d_packed, kept_one, sent_one = call(
        plain_kernel,
        "backward_plain",
        (field, packed_field, half, half),
        core, keep, tall, side, corner, proj_weights, join, packed, probs, mixed, normed,
        scratch=[(TOKENS, D), (32, 64, D)],
        scalar=True,
        fetch={6: None, 5: 0, 7: None, 8: None, 10: None, 9: None},
        store=(0, 1, 2, 3),
        limit=51,
        micros=10,
    )
    d_tokens = call(
        finish_kernel,
        "finish_plain",
        field,
        values, gradient, d_packed, qkv_weights, unplain,
        fetch={2: None, 3: 0, 0: None, 1: None, 4: None},
        limit=LARGE,
        micros=5,
    )
    sent_one, parts_two = lax.optimization_barrier((sent_one, parts_two))
    chunks_one = core_reduced(kept_one, sent_one)
    d_tokens, grad_qkv, grad_proj = reduced(chunks_one, parts_two, d_tokens)
    return d_tokens.reshape(tokens.shape), grad_qkv, grad_proj


def solution(mesh):
    return jax.shard_map(
        body,
        mesh=mesh,
        in_specs=(P(None, "lat", "lon", None), P(None, "lat", "lon", None), P(), P()),
        out_specs=(P(None, "lat", "lon", None), P(None, "lat", "lon"), P(None, "lat", "lon")),
        check_vma=False,
    )
```

```python
import functools

import jax
import jax.numpy as jnp
import numpy as np
from jax import lax
from jax.experimental import pallas as pl
from jax.experimental.pallas import tpu as pltpu
from jax.sharding import PartitionSpec as P

D = 512
HEADS = 8
HEAD_DIM = 64
LEVELS = 2
WIN_LAT = 12
WIN_LON = 6
HALF_LAT = 6
HALF_LON = 3
ROWS = 12
COLS = 24
TOKENS = LEVELS * ROWS * COLS
WINDOW = LEVELS * WIN_LAT * WIN_LON
WINDOWS = TOKENS // WINDOW
HALF = TOKENS // 2
QUAD = 4 * HEAD_DIM
LEVEL = ROWS * COLS
SEGMENT = WIN_LAT * WIN_LON
WIDE = 128
STRIP = 32
PIECES = 2 * WIDE + 2 * STRIP
EPSILON = 1e-05
MASKED = -1000000000.0
SCALE = HEAD_DIM ** (-0.5)
LARGE = 58
SMALL = 6
PEAK_FLOPS = 1_150_000_000
PEAK_BYTES = 3_690_000
F32 = jnp.float32
BF16 = jnp.bfloat16


def window_order(row, col):
    return (col // WIN_LON) * SEGMENT + row * WIN_LON + col % WIN_LON


def field_order(row, col):
    return row * COLS + col


def piece_order(row, col):
    upper = int(row < HALF_LAT)
    at = row % HALF_LAT
    if col < HALF_LON:
        return 2 * WIDE + STRIP * upper + at * HALF_LON + col
    return WIDE * upper + at * (COLS - HALF_LON) + col - HALF_LON


def half_order(row, col):
    if col >= COLS:
        return LEVEL + piece_order(row, col - COLS) - 2 * WIDE
    return LEVEL // 2 * int(row < HALF_LAT) + (row % HALF_LAT) * COLS + col


def selection(shape, pairs):
    out = np.zeros(shape, np.float32)
    for row, column in pairs:
        out[row, column] = 1
    return jnp.asarray(out, BF16)


CELLS = list(np.ndindex(ROWS, COLS))
PLAIN = [(window_order(*cell), field_order(*cell)) for cell in CELLS]
JOIN = [(window_order(*cell), piece_order(*cell)) for cell in CELLS]
STRIPS = [(piece_order(*cell) - 2 * WIDE, field_order(*cell)) for cell in CELLS if cell[1] < HALF_LON]
SHIFTED = [((r + HALF_LAT) % ROWS, c + HALF_LON) for r, c in CELLS]
SHIFT = [(window_order(*cell), piece_order(r, c % COLS)) for cell, (r, c) in zip(CELLS, SHIFTED)]
SHIFT_HALF = [(window_order(*cell), half_order(r, c)) for cell, (r, c) in zip(CELLS, SHIFTED)]


def flipped(pairs):
    return [(column, row) for row, column in pairs]


class Fetched:
    def __init__(self, source, target, sem):
        self.copy, self.target, self.waiting = pltpu.make_async_copy(source, target, sem), target, True
        self.copy.start()

    def __getitem__(self, index):
        if self.waiting:
            self.copy.wait()
            self.waiting = False
        return self.target[index]


class Stored:
    def __init__(self, source, target, sem):
        self.copy, self.source = pltpu.make_async_copy(source, target, sem), source

    def __getitem__(self, index):
        return self.source[index]

    def __setitem__(self, index, value):
        self.source[index] = value

    def flush(self):
        self.copy.start()


def dot(a, b):
    return lax.dot_general(a, b, (((1,), (0,)), ((), ())), preferred_element_type=F32)


def dot_nt(a, b):
    return lax.dot_general(a, b, (((1,), (1,)), ((), ())), preferred_element_type=F32)


def dot_tn(a, b):
    return lax.dot_general(a, b, (((0,), (0,)), ((), ())), preferred_element_type=F32)


def gathered(matrix, levels):
    parts = [dot(matrix[...], level) for level in levels]
    segments = [part[w * SEGMENT : (w + 1) * SEGMENT] for w in range(WINDOWS) for part in parts]
    return jnp.concatenate(segments, axis=0)


def scattered(matrix, values):
    parts = []
    for level in range(LEVELS):
        starts = [w * WINDOW + level * SEGMENT for w in range(WINDOWS)]
        own = jnp.concatenate([values[start : start + SEGMENT] for start in starts], axis=0)
        parts.append(dot(matrix[...], own.astype(BF16)).astype(BF16))
    return parts


def pieces_of(refs, strip_at=0):
    out = []
    for level in range(LEVELS):
        strip_start = strip_at + level * STRIP
        spans = [slice(level * WIDE, (level + 1) * WIDE)] * 2 + [slice(strip_start, strip_start + STRIP)] * 2
        out.append(jnp.concatenate([ref[span] for ref, span in zip(refs, spans)], axis=0))
    return out


def put_pieces(parts, refs):
    for level, part in enumerate(parts):
        at = 0
        for ref, size in zip(refs, (WIDE, WIDE, STRIP, STRIP)):
            ref[level * size : (level + 1) * size] = part[at : at + size]
            at += size


def layer_norm(values):
    centred = values - jnp.mean(values, axis=-1, keepdims=True)
    inverse = lax.rsqrt(jnp.mean(centred * centred, axis=-1, keepdims=True) + EPSILON)
    return centred * inverse, inverse


def stacked(part, scale):
    lane = lax.broadcasted_iota(jnp.int32, (1, QUAD), 1) // HEAD_DIM
    wide = [part * jnp.where(lane == h, scale, 0.0).astype(BF16) for h in range(4)]
    return jnp.concatenate(wide, axis=0)


def unstacked(product):
    lane = lax.broadcasted_iota(jnp.int32, (WINDOW, QUAD), 1) // HEAD_DIM
    out = product[:WINDOW]
    for h in range(1, 4):
        out = jnp.where(lane == h, product[h * WINDOW : (h + 1) * WINDOW], out)
    return out


def soft(keys_stacked, queries, bias):
    out = []
    for h in range(4):
        scores = dot_nt(keys_stacked[h * WINDOW : (h + 1) * WINDOW], queries)
        if bias is not None:
            scores = scores + bias
        raised = jnp.exp(scores - jnp.max(scores, axis=0, keepdims=True))
        out.append(raised * (1.0 / jnp.sum(raised, axis=0, keepdims=True)))
    return out


def places(w, quad):
    span = slice(w * WINDOW, (w + 1) * WINDOW)
    return span, [slice(n * D + quad * QUAD, n * D + (quad + 1) * QUAD) for n in range(3)]


def forward_kernel(
    tokens, cotangent, w_qkv, w_proj, plain, cut, strips,
    keep, tall, side, corner, values_out, normed_out, packed, probs_out, mixed,
):
    values = gathered(plain, [tokens[:LEVEL], tokens[LEVEL:]])
    values_out[...] = values.astype(BF16)
    values_out.flush()
    normed = layer_norm(values)[0].astype(BF16)
    normed_out[...] = normed
    normed_out.flush()
    packed[...] = dot(normed, w_qkv[...]).astype(BF16)
    packed.flush()
    for w in range(WINDOWS):
        for quad in range(2):
            span, at = places(w, quad)
            queries, keys, vals = [packed[span, at[n]] for n in range(3)]
            probs = jnp.concatenate(soft(stacked(keys, SCALE), queries, None), axis=0).astype(BF16)
            probs_out[2 * w + quad] = probs
            mixed[span, at[0]] = dot_tn(probs, stacked(vals, 1.0)).astype(BF16)
    probs_out.flush()
    mixed.flush()
    first = values + dot(mixed[...], w_proj[...])
    put_pieces(scattered(cut, first), (keep, tall, side, corner))
    for level in range(LEVELS):
        part = dot(strips[...], cotangent[level * LEVEL : (level + 1) * LEVEL]).astype(BF16)
        at = slice((LEVELS + level) * STRIP, (LEVELS + level + 1) * STRIP)
        side[at] = part[:STRIP]
        corner[at] = part[STRIP:]


def attention_backward(packed, probs, probs_low, d_mixed, d_packed, span, at, keys_stacked, vals_stacked):
    d_scores = []
    for h in range(4):
        d_probs = dot_nt(vals_stacked[h * WINDOW : (h + 1) * WINDOW], d_mixed)
        inner = jnp.sum(probs[h] * d_probs, axis=0, keepdims=True)
        d_scores.append((probs[h] * (d_probs - inner)).astype(BF16))
    d_scores = jnp.concatenate(d_scores, axis=0)
    d_packed[span, at[0]] = dot_tn(d_scores, keys_stacked).astype(BF16)
    d_packed[span, at[1]] = (unstacked(dot(d_scores, packed[span, at[0]])) * SCALE).astype(BF16)
    d_packed[span, at[2]] = unstacked(dot(probs_low, d_mixed)).astype(BF16)


def input_gradient(values, gradient, d_packed, w_qkv):
    standard, inverse = layer_norm(values)
    d_normed = dot_nt(d_packed, w_qkv)
    d_input = inverse * (
        d_normed
        - jnp.mean(d_normed, axis=-1, keepdims=True)
        - standard * jnp.mean(d_normed * standard, axis=-1, keepdims=True)
    )
    return gradient.astype(F32) + d_input


def weight_gradients(core, normed, d_packed, mixed, gradient, grads, kept, sent):
    grads[:, :48] = dot_tn(d_packed, normed).astype(BF16).reshape(32, 48, D)
    grads[:, 48:] = dot_tn(gradient, mixed).astype(BF16).reshape(32, 16, D)
    for j in range(16):
        kept[j] = grads[2 * j + core[0]]
        sent[j] = grads[2 * j + 1 - core[0]]


def shifted_kernel(
    core, keep, tall, side, corner, cotangent, tall_g, w_qkv, w_proj, gather, gather_g, scatter, bias,
    keep_out, tall_out, side_out, corner_out, kept, sent,
    packed, d_mixed_all, mixed, d_packed, grads,
):
    sources = []
    for level in range(LEVELS):
        own = cotangent[level * LEVEL + LEVEL // 2 : (level + 1) * LEVEL]
        beside = [ref[(LEVELS + level) * STRIP : (LEVELS + level + 1) * STRIP] for ref in (side, corner)]
        sources.append(
            jnp.concatenate([own, tall_g[level * (LEVEL // 2) : (level + 1) * (LEVEL // 2)], *beside], axis=0)
        )
    gradient = gathered(gather_g, sources).astype(BF16)
    d_mixed_all[...] = dot_nt(gradient, w_proj[...]).astype(BF16)
    values = gathered(gather, pieces_of((keep, tall, side, corner)))
    normed = layer_norm(values)[0].astype(BF16)
    packed[...] = dot(normed, w_qkv[...]).astype(BF16)
    for w in range(WINDOWS):
        for quad in range(2):
            span, at = places(w, quad)
            queries, keys, vals = [packed[span, at[n]] for n in range(3)]
            keys_stacked, vals_stacked = stacked(keys, SCALE), stacked(vals, 1.0)
            probs = soft(keys_stacked, queries, bias[...])
            probs_low = jnp.concatenate(probs, axis=0).astype(BF16)
            mixed[span, at[0]] = dot_tn(probs_low, vals_stacked).astype(BF16)
            attention_backward(
                packed, probs, probs_low, d_mixed_all[span, at[0]], d_packed, span, at, keys_stacked, vals_stacked
            )
    weight_gradients(core, normed, d_packed[...], mixed[...], gradient, grads, kept, sent)
    kept.flush()
    sent.flush()
    result = input_gradient(values, gradient, d_packed[...], w_qkv[...])
    put_pieces(scattered(scatter, result), (keep_out, tall_out, side_out, corner_out))


def plain_kernel(
    core, keep, tall, side, corner, w_proj, join, packed, probs_in, mixed, normed,
    gradient_out, d_packed, kept, sent,
    d_mixed_all, grads,
):
    gradient = gathered(join, pieces_of((keep, tall, side, corner))).astype(BF16)
    gradient_out[...] = gradient
    gradient_out.flush()
    d_mixed_all[...] = dot_nt(gradient, w_proj[...]).astype(BF16)
    for w in range(WINDOWS):
        for quad in range(2):
            span, at = places(w, quad)
            keys_stacked, vals_stacked = stacked(packed[span, at[1]], SCALE), stacked(packed[span, at[2]], 1.0)
            probs_low = probs_in[2 * w + quad]
            probs = [probs_low[h * WINDOW : (h + 1) * WINDOW].astype(F32) for h in range(4)]
            attention_backward(
                packed, probs, probs_low, d_mixed_all[span, at[0]], d_packed, span, at, keys_stacked, vals_stacked
            )
    d_packed.flush()
    weight_gradients(core, normed[...], d_packed[...], mixed[...], gradient, grads, kept, sent)
    kept.flush()
    sent.flush()


def finish_kernel(values, gradient, d_packed, w_qkv, unplain, d_tokens):
    result = input_gradient(values[...].astype(F32), gradient[...], d_packed[...], w_qkv[...])
    for level, part in enumerate(scattered(unplain, result)):
        d_tokens[level * LEVEL : (level + 1) * LEVEL] = part


def swapped_halves(top, bottom):
    left = lax.broadcasted_iota(jnp.int32, top.shape, 1) < top.shape[1] // 2
    turned = [pltpu.roll(x, top.shape[1] // 2, 1) for x in (top, bottom)]
    return jnp.where(left, top, turned[1]), jnp.where(left, turned[0], bottom)


def core_sums(kept, received, landing, sems):
    half = kept.shape[0] // 2
    spans = [slice(pair * 128, (pair + 1) * 128) for pair in range(4)]
    copies = [pltpu.make_async_copy(kept.at[:, at], landing.at[n], sems.at[n]) for n, at in enumerate(spans)]
    for copy in copies:
        copy.start()
    for pair, at in enumerate(spans):
        copies[pair].wait()
        total = landing[pair].astype(F32) + received[:, at].astype(F32)
        for odd, part in enumerate(swapped_halves(total[:half], total[half:])):
            yield 2 * pair + odd, part.astype(BF16)


def core_sum_kernel(kept, received, out, landing, made, sems):
    leaving = []
    for lat, part in core_sums(kept, received, landing, sems):
        made[lat] = part
        leaving.append(pltpu.make_async_copy(made.at[lat], out.at[lat], sems.at[4 + lat]))
        leaving[-1].start()
    for copy in leaving:
        copy.wait()


def core_cut_kernel(place, kept, received, *refs):
    outs, (landing, held, sems) = refs[:-3], refs[-3:]
    for lat, part in core_sums(kept, received, landing, sems):
        held[lat // 2, lat % 2] = part
    for step, out in enumerate(outs):
        out[...] = held[lax.rem(place[0] + step, 4)]


def far_sum_kernel(place, one, two, three, four, kept, sent):
    total = one[...].astype(F32) + two[...].astype(F32) + three[...].astype(F32) + four[...].astype(F32)
    first = place[0] == 0
    kept[...] = jnp.where(first, total[0], total[1]).astype(BF16)
    sent[...] = jnp.where(first, total[1], total[0]).astype(BF16)


def lat_sum_kernel(parts, kept, received, out):
    total = parts[0].astype(F32)
    for a in range(1, 8):
        total = total + parts[a].astype(F32)
    other = kept[...].astype(F32) + received[...].astype(F32)
    for block, held in enumerate((total, other)):
        for j in range(8):
            low, high = swapped_halves(held[64 * j : 64 * j + 32], held[64 * j + 32 : 64 * j + 64])
            out[j, block] = low.astype(BF16)
            out[j + 8, block] = high.astype(BF16)


def lon_sum_kernel(parts, grad_qkv, grad_proj):
    for block in range(2):
        total = parts[0, block].astype(F32)
        for j in range(1, 16):
            total = total + parts[j, block].astype(F32)
        whole = jnp.concatenate([total, pltpu.roll(total, 64, 1)], axis=0)
        grad_qkv[block] = whole[:48, :64]
        grad_proj[block] = whole[48:, :64]


def shape(*dims, kind=BF16):
    return jax.ShapeDtypeStruct(dims, kind)


def call(kernel, name, outs, *operands, scratch=(), scalar=False, fetch=None, store=(), apart=(), own_out=False, limit=SMALL, micros=1):
    fetch = fetch or {}
    several = outs if isinstance(outs, tuple) else (outs,)
    cut = np.cumsum([0, len(operands), len(several), len(scratch), len(fetch), len(store)])

    def body(*refs):
        ins, results, own, landing, leaving = [list(refs[a:b]) for a, b in zip(cut[:-1], cut[1:])]
        for at, (n, index) in enumerate(fetch.items()):
            ins[n] = Fetched(ins[n] if index is None else ins[n].at[index], landing[at], refs[-2].at[at])
        for at, n in enumerate(store):
            results[n] = Stored(leaving[at], results[n], refs[-1].at[at])
        kernel(*ins, *results, *own)
        for n in store:
            results[n].copy.wait()

    held = [pltpu.VMEM(dims, BF16) if isinstance(dims, tuple) else dims for dims in scratch]
    for n, index in fetch.items():
        held.append(pltpu.VMEM(operands[n].shape if index is None else operands[n].shape[1:], BF16))
    held += [pltpu.VMEM(several[n].shape, BF16) for n in store]
    if fetch or store:
        held += [pltpu.SemaphoreType.DMA((max(1, len(group)),)) for group in (fetch, store)]
    kinds = [pltpu.HBM if n in fetch or n in apart else pltpu.VMEM for n in range(len(operands))]
    if scalar:
        kinds[0] = pltpu.SMEM
    specs = tuple(pl.BlockSpec(memory_space=pltpu.HBM if own_out or n in store else pltpu.VMEM) for n in range(len(several)))
    return pl.pallas_call(
        body,
        out_shape=outs,
        in_specs=[pl.BlockSpec(memory_space=kind) for kind in kinds],
        out_specs=specs if isinstance(outs, tuple) else specs[0],
        scratch_shapes=held,
        compiler_params=pltpu.CompilerParams(vmem_limit_bytes=limit * 1024 * 1024),
        cost_estimate=pl.CostEstimate(
            flops=micros * PEAK_FLOPS, bytes_accessed=micros * PEAK_BYTES, transcendentals=0
        ),
        name=name,
    )(*operands)


def moved(piece, lat, lon):
    n_lat, n_lon = lax.axis_size("lat"), lax.axis_size("lon")
    if lon == 0:
        return lax.ppermute(piece, "lat", [(i, (i + lat) % n_lat) for i in range(n_lat)])
    if lat == 0:
        return lax.ppermute(piece, "lon", [(i, (i + lon) % n_lon) for i in range(n_lon)])
    route = [
        (a * n_lon + b, (a + lat) % n_lat * n_lon + (b + lon) % n_lon)
        for a in range(n_lat)
        for b in range(n_lon)
    ]
    return lax.ppermute(piece, ("lat", "lon"), route)


def exchanged(tall, side, corner, step):
    corner = moved(corner, step, step)
    side = moved(side, 0, step)
    return moved(tall, step, 0), side, corner


def core_swapped(sent):
    return lax.ppermute(sent, "lon", [(i, i ^ 1) for i in range(lax.axis_size("lon"))]).reshape(1024, D)


def core_reduced(kept, sent):
    return call(
        core_sum_kernel, "core_sum", shape(8, 512, 128), kept.reshape(1024, D), core_swapped(sent),
        scratch=[(4, 1024, 128), (8, 512, 128), pltpu.SemaphoreType.DMA((12,))], apart=(0,), own_out=True, limit=12,
    )


def core_cut(kept, sent):
    place = (lax.axis_index("lat") // 2).astype(jnp.int32).reshape(1)
    return call(
        core_cut_kernel, "core_cut", (shape(2, 512, 128),) * 4, place, kept.reshape(1024, D), core_swapped(sent),
        scratch=[(4, 1024, 128), (4, 2, 512, 128), pltpu.SemaphoreType.DMA((4,))], scalar=True, apart=(1,), limit=12,
    )


def far_reduced(parts):
    n = lax.axis_size("lat")
    arrived = [parts[0]]
    for step in (2, 3, 1):
        arrived.append(lax.ppermute(parts[step], "lat", [(i, (i + 2 * step) % n) for i in range(n)]))
    place = (lax.axis_index("lat") % 2).astype(jnp.int32).reshape(1)
    kept, sent = call(far_sum_kernel, "far_sum", (shape(512, 128),) * 2, place, *arrived, scalar=True)
    return kept, sent


def reduced(chunks_one, parts_two, d_tokens):
    kept, sent = parts_two
    received = lax.ppermute(sent, "lat", [(i, i ^ 1) for i in range(lax.axis_size("lat"))])
    chunks_one, received = lax.optimization_barrier((chunks_one, received))
    arrived = lax.all_to_all(chunks_one, "lat", 0, 0, tiled=True)
    arrived, d_tokens = lax.optimization_barrier((arrived, d_tokens))
    both = call(lat_sum_kernel, "lat_sum", shape(16, 2, 32, 128), arrived, kept, received)
    groups = [[2 * j + core for j in range(16)] for core in range(2)]
    arrived = lax.all_to_all(both, "lon", 0, 0, tiled=True, axis_index_groups=groups)
    grads = call(lon_sum_kernel, "lon_sum", (shape(2, 48, 64, kind=F32), shape(2, 16, 64, kind=F32)), arrived)
    return d_tokens, *[grad.transpose(0, 2, 1) for grad in grads]


def body(tokens, cotangent, qkv_weights, proj_weights):
    plain, unplain = selection((LEVEL, LEVEL), PLAIN), selection((LEVEL, LEVEL), flipped(PLAIN))
    join, cut = selection((LEVEL, PIECES), JOIN), selection((PIECES, LEVEL), flipped(JOIN))
    shift, unshift = selection((LEVEL, PIECES), SHIFT), selection((PIECES, LEVEL), flipped(SHIFT))
    shift_half, strips = selection((LEVEL, LEVEL + 2 * STRIP), SHIFT_HALF), selection((2 * STRIP, LEVEL), STRIPS)
    core = (lax.axis_index("lon") % 2).astype(jnp.int32).reshape(1)
    last_lat = lax.axis_index("lat") == lax.axis_size("lat") - 1
    label = (np.arange(WINDOW) // WIN_LON % WIN_LAT >= HALF_LAT).astype(np.int32)
    bias = jnp.where(last_lat & (label[:, None] != label[None, :]), MASKED, 0.0).astype(F32)
    field, flat = shape(TOKENS, D), tokens.reshape(TOKENS, D)
    wide, strip, pair = [shape(LEVELS * rows, D) for rows in (WIDE, STRIP, 2 * STRIP)]
    packed_field = shape(TOKENS, 3 * D)
    half = shape(16, 64, D)

    tall_g = moved(cotangent[:, :HALF_LAT].reshape(HALF, D), -1, 0)
    flat_g = cotangent.reshape(TOKENS, D)
    keep, tall, side, corner, values, normed, packed, probs, mixed = call(
        forward_kernel,
        "forward",
        (wide, wide, pair, pair, field, field, packed_field, shape(2 * WINDOWS, 4 * WINDOW, WINDOW), field),
        flat, flat_g, qkv_weights, proj_weights, plain, cut, strips,
        fetch={4: None, 0: None, 2: 0, 3: 0, 5: None, 6: None, 1: None},
        store=(4, 5, 6, 7, 8),
        limit=58,
        micros=9,
    )
    tall, side, corner = exchanged(tall, side, corner, -1)
    keep, tall, side, corner, kept_two, sent_two = call(
        shifted_kernel,
        "backward_shifted",
        (wide, wide, strip, strip, half, half),
        core, keep, tall, side, corner, flat_g, tall_g, qkv_weights, proj_weights, shift, shift_half, unshift, bias,
        scratch=[(TOKENS, 3 * D), (TOKENS, D), (TOKENS, D), (TOKENS, 3 * D), (32, 64, D)],
        scalar=True,
        fetch={5: None, 10: None, 8: 1, 9: None, 7: 1, 11: None},
        store=(4, 5),
        limit=51,
        micros=18,
    )
    tall, side, corner = exchanged(tall, side, corner, 1)
    parts_two = far_reduced(core_cut(kept_two, sent_two))
    gradient, d_packed, kept_one, sent_one = call(
        plain_kernel,
        "backward_plain",
        (field, packed_field, half, half),
        core, keep, tall, side, corner, proj_weights, join, packed, probs, mixed, normed,
        scratch=[(TOKENS, D), (32, 64, D)],
        scalar=True,
        fetch={6: None, 5: 0, 7: None, 8: None, 10: None, 9: None},
        store=(0, 1, 2, 3),
        limit=53,
        micros=10,
    )
    d_tokens = call(
        finish_kernel,
        "finish_plain",
        field,
        values, gradient, d_packed, qkv_weights, unplain,
        fetch={2: None, 3: 0, 0: None, 1: None, 4: None},
        limit=LARGE,
        micros=5,
    )
    sent_one, parts_two = lax.optimization_barrier((sent_one, parts_two))
    chunks_one = core_reduced(kept_one, sent_one)
    d_tokens, grad_qkv, grad_proj = reduced(chunks_one, parts_two, d_tokens)
    return d_tokens.reshape(tokens.shape), grad_qkv, grad_proj


def solution(mesh):
    return jax.shard_map(
        body,
        mesh=mesh,
        in_specs=(P(None, "lat", "lon", None), P(None, "lat", "lon", None), P(), P()),
        out_specs=(P(None, "lat", "lon", None), P(None, "lat", "lon"), P(None, "lat", "lon")),
        check_vma=False,
    )
```

```python
import functools

import jax
import jax.numpy as jnp
import numpy as np
from jax import lax
from jax.experimental import pallas as pl
from jax.experimental.pallas import tpu as pltpu
from jax.sharding import PartitionSpec as P

D = 512
HEADS = 8
HEAD_DIM = 64
LEVELS = 2
WIN_LAT = 12
WIN_LON = 6
HALF_LAT = 6
HALF_LON = 3
ROWS = 12
COLS = 24
TOKENS = LEVELS * ROWS * COLS
WINDOW = LEVELS * WIN_LAT * WIN_LON
WINDOWS = TOKENS // WINDOW
HALF = TOKENS // 2
QUAD = 4 * HEAD_DIM
LEVEL = ROWS * COLS
SEGMENT = WIN_LAT * WIN_LON
WIDE = 128
STRIP = 32
PIECES = 2 * WIDE + 2 * STRIP
EPSILON = 1e-05
MASKED = -1000000000.0
SCALE = HEAD_DIM ** (-0.5)
LARGE = 58
SMALL = 6
PEAK_FLOPS = 1_150_000_000
PEAK_BYTES = 3_690_000
F32 = jnp.float32
BF16 = jnp.bfloat16


def window_order(row, col):
    return (col // WIN_LON) * SEGMENT + row * WIN_LON + col % WIN_LON


def field_order(row, col):
    return row * COLS + col


def piece_order(row, col):
    upper = int(row < HALF_LAT)
    at = row % HALF_LAT
    if col < HALF_LON:
        return 2 * WIDE + STRIP * upper + at * HALF_LON + col
    return WIDE * upper + at * (COLS - HALF_LON) + col - HALF_LON


def half_order(row, col):
    if col >= COLS:
        return LEVEL + piece_order(row, col - COLS) - 2 * WIDE
    return LEVEL // 2 * int(row < HALF_LAT) + (row % HALF_LAT) * COLS + col


def selection(shape, pairs):
    out = np.zeros(shape, np.float32)
    for row, column in pairs:
        out[row, column] = 1
    return jnp.asarray(out, BF16)


CELLS = list(np.ndindex(ROWS, COLS))
PLAIN = [(window_order(*cell), field_order(*cell)) for cell in CELLS]
JOIN = [(window_order(*cell), piece_order(*cell)) for cell in CELLS]
STRIPS = [(piece_order(*cell) - 2 * WIDE, field_order(*cell)) for cell in CELLS if cell[1] < HALF_LON]
SHIFTED = [((r + HALF_LAT) % ROWS, c + HALF_LON) for r, c in CELLS]
SHIFT = [(window_order(*cell), piece_order(r, c % COLS)) for cell, (r, c) in zip(CELLS, SHIFTED)]
SHIFT_HALF = [(window_order(*cell), half_order(r, c)) for cell, (r, c) in zip(CELLS, SHIFTED)]


def flipped(pairs):
    return [(column, row) for row, column in pairs]


class Fetched:
    def __init__(self, source, target, sem):
        self.copy, self.target, self.waiting = pltpu.make_async_copy(source, target, sem), target, True
        self.copy.start()

    def __getitem__(self, index):
        if self.waiting:
            self.copy.wait()
            self.waiting = False
        return self.target[index]


class Stored:
    def __init__(self, source, target, sem):
        self.copy, self.source = pltpu.make_async_copy(source, target, sem), source

    def __getitem__(self, index):
        return self.source[index]

    def __setitem__(self, index, value):
        self.source[index] = value

    def flush(self):
        self.copy.start()


def dot(a, b):
    return lax.dot_general(a, b, (((1,), (0,)), ((), ())), preferred_element_type=F32)


def dot_nt(a, b):
    return lax.dot_general(a, b, (((1,), (1,)), ((), ())), preferred_element_type=F32)


def dot_tn(a, b):
    return lax.dot_general(a, b, (((0,), (0,)), ((), ())), preferred_element_type=F32)


def gathered(matrix, levels):
    parts = [dot(matrix[...], level) for level in levels]
    segments = [part[w * SEGMENT : (w + 1) * SEGMENT] for w in range(WINDOWS) for part in parts]
    return jnp.concatenate(segments, axis=0)


def scattered(matrix, values):
    parts = []
    for level in range(LEVELS):
        starts = [w * WINDOW + level * SEGMENT for w in range(WINDOWS)]
        own = jnp.concatenate([values[start : start + SEGMENT] for start in starts], axis=0)
        parts.append(dot(matrix[...], own.astype(BF16)).astype(BF16))
    return parts


def pieces_of(refs, strip_at=0):
    out = []
    for level in range(LEVELS):
        strip_start = strip_at + level * STRIP
        spans = [slice(level * WIDE, (level + 1) * WIDE)] * 2 + [slice(strip_start, strip_start + STRIP)] * 2
        out.append(jnp.concatenate([ref[span] for ref, span in zip(refs, spans)], axis=0))
    return out


def put_pieces(parts, refs):
    for level, part in enumerate(parts):
        at = 0
        for ref, size in zip(refs, (WIDE, WIDE, STRIP, STRIP)):
            ref[level * size : (level + 1) * size] = part[at : at + size]
            at += size


def layer_norm(values):
    centred = values - jnp.mean(values, axis=-1, keepdims=True)
    inverse = lax.rsqrt(jnp.mean(centred * centred, axis=-1, keepdims=True) + EPSILON)
    return centred * inverse, inverse


def stacked(part, scale):
    lane = lax.broadcasted_iota(jnp.int32, (1, QUAD), 1) // HEAD_DIM
    wide = [part * jnp.where(lane == h, scale, 0.0).astype(BF16) for h in range(4)]
    return jnp.concatenate(wide, axis=0)


def unstacked(product):
    lane = lax.broadcasted_iota(jnp.int32, (WINDOW, QUAD), 1) // HEAD_DIM
    out = product[:WINDOW]
    for h in range(1, 4):
        out = jnp.where(lane == h, product[h * WINDOW : (h + 1) * WINDOW], out)
    return out


def soft(keys_stacked, queries, bias):
    out = []
    for h in range(4):
        scores = dot_nt(keys_stacked[h * WINDOW : (h + 1) * WINDOW], queries)
        if bias is not None:
            scores = scores + bias
        raised = jnp.exp(scores - jnp.max(scores, axis=0, keepdims=True))
        out.append(raised * (1.0 / jnp.sum(raised, axis=0, keepdims=True)))
    return out


def places(w, quad):
    span = slice(w * WINDOW, (w + 1) * WINDOW)
    return span, [slice(n * D + quad * QUAD, n * D + (quad + 1) * QUAD) for n in range(3)]


def forward_kernel(
    tokens, cotangent, w_qkv, w_proj, plain, cut, strips,
    keep, tall, side, corner, values_out, normed_out, packed, probs_out, mixed,
):
    values = gathered(plain, [tokens[:LEVEL], tokens[LEVEL:]])
    values_out[...] = values.astype(BF16)
    values_out.flush()
    normed = layer_norm(values)[0].astype(BF16)
    normed_out[...] = normed
    normed_out.flush()
    packed[...] = dot(normed, w_qkv[...]).astype(BF16)
    packed.flush()
    for w in range(WINDOWS):
        for quad in range(2):
            span, at = places(w, quad)
            queries, keys, vals = [packed[span, at[n]] for n in range(3)]
            probs = jnp.concatenate(soft(stacked(keys, SCALE), queries, None), axis=0).astype(BF16)
            probs_out[2 * w + quad] = probs
            mixed[span, at[0]] = dot_tn(probs, stacked(vals, 1.0)).astype(BF16)
    probs_out.flush()
    mixed.flush()
    first = values + dot(mixed[...], w_proj[...])
    put_pieces(scattered(cut, first), (keep, tall, side, corner))
    for level in range(LEVELS):
        part = dot(strips[...], cotangent[level * LEVEL : (level + 1) * LEVEL]).astype(BF16)
        at = slice((LEVELS + level) * STRIP, (LEVELS + level + 1) * STRIP)
        side[at] = part[:STRIP]
        corner[at] = part[STRIP:]


def attention_backward(packed, probs, probs_low, d_mixed, d_packed, span, at, keys_stacked, vals_stacked):
    d_scores = []
    for h in range(4):
        d_probs = dot_nt(vals_stacked[h * WINDOW : (h + 1) * WINDOW], d_mixed)
        inner = jnp.sum(probs[h] * d_probs, axis=0, keepdims=True)
        d_scores.append((probs[h] * (d_probs - inner)).astype(BF16))
    d_scores = jnp.concatenate(d_scores, axis=0)
    d_packed[span, at[0]] = dot_tn(d_scores, keys_stacked).astype(BF16)
    d_packed[span, at[1]] = (unstacked(dot(d_scores, packed[span, at[0]])) * SCALE).astype(BF16)
    d_packed[span, at[2]] = unstacked(dot(probs_low, d_mixed)).astype(BF16)


def input_gradient(values, gradient, d_packed, w_qkv):
    standard, inverse = layer_norm(values)
    d_normed = dot_nt(d_packed, w_qkv)
    d_input = inverse * (
        d_normed
        - jnp.mean(d_normed, axis=-1, keepdims=True)
        - standard * jnp.mean(d_normed * standard, axis=-1, keepdims=True)
    )
    return gradient.astype(F32) + d_input


def weight_gradients(core, normed, d_packed, mixed, gradient, grads, kept, sent):
    grads[:, :48] = dot_tn(d_packed, normed).astype(BF16).reshape(32, 48, D)
    grads[:, 48:] = dot_tn(gradient, mixed).astype(BF16).reshape(32, 16, D)
    for j in range(16):
        kept[j] = grads[2 * j + core[0]]
        sent[j] = grads[2 * j + 1 - core[0]]


def shifted_kernel(
    core, keep, tall, side, corner, cotangent, tall_g, w_qkv, w_proj, gather, gather_g, scatter, bias,
    keep_out, tall_out, side_out, corner_out, kept, sent,
    packed, d_mixed_all, mixed, d_packed, grads,
):
    sources = []
    for level in range(LEVELS):
        own = cotangent[level * LEVEL + LEVEL // 2 : (level + 1) * LEVEL]
        beside = [ref[(LEVELS + level) * STRIP : (LEVELS + level + 1) * STRIP] for ref in (side, corner)]
        sources.append(
            jnp.concatenate([own, tall_g[level * (LEVEL // 2) : (level + 1) * (LEVEL // 2)], *beside], axis=0)
        )
    gradient = gathered(gather_g, sources).astype(BF16)
    d_mixed_all[...] = dot_nt(gradient, w_proj[...]).astype(BF16)
    values = gathered(gather, pieces_of((keep, tall, side, corner)))
    normed = layer_norm(values)[0].astype(BF16)
    packed[...] = dot(normed, w_qkv[...]).astype(BF16)
    for w in range(WINDOWS):
        for quad in range(2):
            span, at = places(w, quad)
            queries, keys, vals = [packed[span, at[n]] for n in range(3)]
            keys_stacked, vals_stacked = stacked(keys, SCALE), stacked(vals, 1.0)
            probs = soft(keys_stacked, queries, bias[...])
            probs_low = jnp.concatenate(probs, axis=0).astype(BF16)
            mixed[span, at[0]] = dot_tn(probs_low, vals_stacked).astype(BF16)
            attention_backward(
                packed, probs, probs_low, d_mixed_all[span, at[0]], d_packed, span, at, keys_stacked, vals_stacked
            )
    weight_gradients(core, normed, d_packed[...], mixed[...], gradient, grads, kept, sent)
    kept.flush()
    sent.flush()
    result = input_gradient(values, gradient, d_packed[...], w_qkv[...])
    put_pieces(scattered(scatter, result), (keep_out, tall_out, side_out, corner_out))


def plain_kernel(
    core, keep, tall, side, corner, w_proj, join, packed, probs_in, mixed, normed,
    gradient_out, d_packed, kept, sent,
    d_mixed_all, grads,
):
    gradient = gathered(join, pieces_of((keep, tall, side, corner))).astype(BF16)
    gradient_out[...] = gradient
    gradient_out.flush()
    d_mixed_all[...] = dot_nt(gradient, w_proj[...]).astype(BF16)
    for w in range(WINDOWS):
        for quad in range(2):
            span, at = places(w, quad)
            keys_stacked, vals_stacked = stacked(packed[span, at[1]], SCALE), stacked(packed[span, at[2]], 1.0)
            probs_low = probs_in[2 * w + quad]
            probs = [probs_low[h * WINDOW : (h + 1) * WINDOW].astype(F32) for h in range(4)]
            attention_backward(
                packed, probs, probs_low, d_mixed_all[span, at[0]], d_packed, span, at, keys_stacked, vals_stacked
            )
    d_packed.flush()
    weight_gradients(core, normed[...], d_packed[...], mixed[...], gradient, grads, kept, sent)
    kept.flush()
    sent.flush()


def finish_kernel(values, gradient, d_packed, w_qkv, unplain, d_tokens):
    result = input_gradient(values[...].astype(F32), gradient[...], d_packed[...], w_qkv[...])
    for level, part in enumerate(scattered(unplain, result)):
        d_tokens[level * LEVEL : (level + 1) * LEVEL] = part


def swapped_halves(top, bottom):
    left = lax.broadcasted_iota(jnp.int32, top.shape, 1) < top.shape[1] // 2
    turned = [pltpu.roll(x, top.shape[1] // 2, 1) for x in (top, bottom)]
    return jnp.where(left, top, turned[1]), jnp.where(left, turned[0], bottom)


def core_sums(kept, received):
    half = kept.shape[0] // 2
    for pair in range(4):
        at = slice(pair * 128, (pair + 1) * 128)
        total = kept[:, at].astype(F32) + received[:, at].astype(F32)
        for odd, part in enumerate(swapped_halves(total[:half], total[half:])):
            yield 2 * pair + odd, part.astype(BF16)


def core_sum_kernel(kept, received, out, made, sems):
    leaving = []
    for lat, part in core_sums(kept, received):
        made[lat] = part
        leaving.append(pltpu.make_async_copy(made.at[lat], out.at[lat], sems.at[lat]))
        leaving[-1].start()
    for copy in leaving:
        copy.wait()


def core_cut_kernel(place, kept, received, *refs):
    outs, held = refs[:-1], refs[-1]
    for lat, part in core_sums(kept, received):
        held[lat // 2, lat % 2] = part
    for step, out in enumerate(outs):
        out[...] = held[lax.rem(place[0] + step, 4)]


def far_sum_kernel(place, one, two, three, four, kept, sent):
    total = one[...].astype(F32) + two[...].astype(F32) + three[...].astype(F32) + four[...].astype(F32)
    first = place[0] == 0
    kept[...] = jnp.where(first, total[0], total[1]).astype(BF16)
    sent[...] = jnp.where(first, total[1], total[0]).astype(BF16)


def lat_sum_kernel(parts, kept, received, out):
    total = parts[0].astype(F32)
    for a in range(1, 8):
        total = total + parts[a].astype(F32)
    other = kept[...].astype(F32) + received[...].astype(F32)
    for block, held in enumerate((total, other)):
        for j in range(8):
            low, high = swapped_halves(held[64 * j : 64 * j + 32], held[64 * j + 32 : 64 * j + 64])
            out[j, block] = low.astype(BF16)
            out[j + 8, block] = high.astype(BF16)


def lon_sum_kernel(parts, grad_qkv, grad_proj):
    for block in range(2):
        total = parts[0, block].astype(F32)
        for j in range(1, 16):
            total = total + parts[j, block].astype(F32)
        whole = jnp.concatenate([total, pltpu.roll(total, 64, 1)], axis=0)
        grad_qkv[block] = whole[:48, :64]
        grad_proj[block] = whole[48:, :64]


def shape(*dims, kind=BF16):
    return jax.ShapeDtypeStruct(dims, kind)


def call(kernel, name, outs, *operands, scratch=(), scalar=False, fetch=None, store=(), apart=(), own_out=False, limit=SMALL, micros=1):
    fetch = fetch or {}
    several = outs if isinstance(outs, tuple) else (outs,)
    cut = np.cumsum([0, len(operands), len(several), len(scratch), len(fetch), len(store)])

    def body(*refs):
        ins, results, own, landing, leaving = [list(refs[a:b]) for a, b in zip(cut[:-1], cut[1:])]
        for at, (n, index) in enumerate(fetch.items()):
            ins[n] = Fetched(ins[n] if index is None else ins[n].at[index], landing[at], refs[-2].at[at])
        for at, n in enumerate(store):
            results[n] = Stored(leaving[at], results[n], refs[-1].at[at])
        kernel(*ins, *results, *own)
        for n in store:
            results[n].copy.wait()

    held = [pltpu.VMEM(dims, BF16) if isinstance(dims, tuple) else dims for dims in scratch]
    for n, index in fetch.items():
        held.append(pltpu.VMEM(operands[n].shape if index is None else operands[n].shape[1:], BF16))
    held += [pltpu.VMEM(several[n].shape, BF16) for n in store]
    if fetch or store:
        held += [pltpu.SemaphoreType.DMA((max(1, len(group)),)) for group in (fetch, store)]
    kinds = [pltpu.HBM if n in fetch or n in apart else pltpu.VMEM for n in range(len(operands))]
    if scalar:
        kinds[0] = pltpu.SMEM
    specs = tuple(pl.BlockSpec(memory_space=pltpu.HBM if own_out or n in store else pltpu.VMEM) for n in range(len(several)))
    return pl.pallas_call(
        body,
        out_shape=outs,
        in_specs=[pl.BlockSpec(memory_space=kind) for kind in kinds],
        out_specs=specs if isinstance(outs, tuple) else specs[0],
        scratch_shapes=held,
        compiler_params=pltpu.CompilerParams(vmem_limit_bytes=limit * 1024 * 1024),
        cost_estimate=pl.CostEstimate(
            flops=micros * PEAK_FLOPS, bytes_accessed=micros * PEAK_BYTES, transcendentals=0
        ),
        name=name,
    )(*operands)


def moved(piece, lat, lon):
    n_lat, n_lon = lax.axis_size("lat"), lax.axis_size("lon")
    if lon == 0:
        return lax.ppermute(piece, "lat", [(i, (i + lat) % n_lat) for i in range(n_lat)])
    if lat == 0:
        return lax.ppermute(piece, "lon", [(i, (i + lon) % n_lon) for i in range(n_lon)])
    route = [
        (a * n_lon + b, (a + lat) % n_lat * n_lon + (b + lon) % n_lon)
        for a in range(n_lat)
        for b in range(n_lon)
    ]
    return lax.ppermute(piece, ("lat", "lon"), route)


def exchanged(tall, side, corner, step):
    corner = moved(corner, step, step)
    side = moved(side, 0, step)
    return moved(tall, step, 0), side, corner


def core_swapped(sent):
    return lax.ppermute(sent, "lon", [(i, i ^ 1) for i in range(lax.axis_size("lon"))]).reshape(1024, D)


def core_reduced(kept, sent):
    return call(
        core_sum_kernel, "core_sum", shape(8, 512, 128), kept.reshape(1024, D), core_swapped(sent),
        scratch=[(8, 512, 128), pltpu.SemaphoreType.DMA((8,))], own_out=True, limit=12,
    )


def core_cut(kept, sent):
    place = (lax.axis_index("lat") // 2).astype(jnp.int32).reshape(1)
    return call(
        core_cut_kernel, "core_cut", (shape(2, 512, 128),) * 4, place, kept.reshape(1024, D), core_swapped(sent),
        scratch=[(4, 2, 512, 128)], scalar=True, limit=12,
    )


def far_reduced(parts):
    n = lax.axis_size("lat")
    arrived = [parts[0]]
    for step in (2, 3, 1):
        arrived.append(lax.ppermute(parts[step], "lat", [(i, (i + 2 * step) % n) for i in range(n)]))
    place = (lax.axis_index("lat") % 2).astype(jnp.int32).reshape(1)
    kept, sent = call(far_sum_kernel, "far_sum", (shape(512, 128),) * 2, place, *arrived, scalar=True)
    return kept, sent


def reduced(chunks_one, parts_two, d_tokens):
    kept, sent = parts_two
    received = lax.ppermute(sent, "lat", [(i, i ^ 1) for i in range(lax.axis_size("lat"))])
    chunks_one, received = lax.optimization_barrier((chunks_one, received))
    arrived = lax.all_to_all(chunks_one, "lat", 0, 0, tiled=True)
    arrived, d_tokens = lax.optimization_barrier((arrived, d_tokens))
    both = call(lat_sum_kernel, "lat_sum", shape(16, 2, 32, 128), arrived, kept, received)
    groups = [[2 * j + core for j in range(16)] for core in range(2)]
    arrived = lax.all_to_all(both, "lon", 0, 0, tiled=True, axis_index_groups=groups)
    grads = call(lon_sum_kernel, "lon_sum", (shape(2, 48, 64, kind=F32), shape(2, 16, 64, kind=F32)), arrived)
    return d_tokens, *[grad.transpose(0, 2, 1) for grad in grads]


def body(tokens, cotangent, qkv_weights, proj_weights):
    plain, unplain = selection((LEVEL, LEVEL), PLAIN), selection((LEVEL, LEVEL), flipped(PLAIN))
    join, cut = selection((LEVEL, PIECES), JOIN), selection((PIECES, LEVEL), flipped(JOIN))
    shift, unshift = selection((LEVEL, PIECES), SHIFT), selection((PIECES, LEVEL), flipped(SHIFT))
    shift_half, strips = selection((LEVEL, LEVEL + 2 * STRIP), SHIFT_HALF), selection((2 * STRIP, LEVEL), STRIPS)
    core = (lax.axis_index("lon") % 2).astype(jnp.int32).reshape(1)
    last_lat = lax.axis_index("lat") == lax.axis_size("lat") - 1
    label = (np.arange(WINDOW) // WIN_LON % WIN_LAT >= HALF_LAT).astype(np.int32)
    bias = jnp.where(last_lat & (label[:, None] != label[None, :]), MASKED, 0.0).astype(F32)
    field, flat = shape(TOKENS, D), tokens.reshape(TOKENS, D)
    wide, strip, pair = [shape(LEVELS * rows, D) for rows in (WIDE, STRIP, 2 * STRIP)]
    packed_field = shape(TOKENS, 3 * D)
    half = shape(16, 64, D)

    tall_g = moved(cotangent[:, :HALF_LAT].reshape(HALF, D), -1, 0)
    flat_g = cotangent.reshape(TOKENS, D)
    keep, tall, side, corner, values, normed, packed, probs, mixed = call(
        forward_kernel,
        "forward",
        (wide, wide, pair, pair, field, field, packed_field, shape(2 * WINDOWS, 4 * WINDOW, WINDOW), field),
        flat, flat_g, qkv_weights, proj_weights, plain, cut, strips,
        fetch={4: None, 0: None, 2: 0, 3: 0, 5: None, 6: None, 1: None},
        store=(4, 5, 6, 7, 8),
        limit=58,
        micros=9,
    )
    tall, side, corner = exchanged(tall, side, corner, -1)
    keep, tall, side, corner, kept_two, sent_two = call(
        shifted_kernel,
        "backward_shifted",
        (wide, wide, strip, strip, half, half),
        core, keep, tall, side, corner, flat_g, tall_g, qkv_weights, proj_weights, shift, shift_half, unshift, bias,
        scratch=[(TOKENS, 3 * D), (TOKENS, D), (TOKENS, D), (TOKENS, 3 * D), (32, 64, D)],
        scalar=True,
        fetch={5: None, 10: None, 8: 1, 9: None, 7: 1, 11: None},
        store=(4, 5),
        limit=51,
        micros=18,
    )
    tall, side, corner = exchanged(tall, side, corner, 1)
    parts_two = far_reduced(core_cut(kept_two, sent_two))
    gradient, d_packed, kept_one, sent_one = call(
        plain_kernel,
        "backward_plain",
        (field, packed_field, half, half),
        core, keep, tall, side, corner, proj_weights, join, packed, probs, mixed, normed,
        scratch=[(TOKENS, D), (32, 64, D)],
        scalar=True,
        fetch={6: None, 5: 0, 7: None, 8: None, 10: None, 9: None},
        store=(0, 1, 2, 3),
        limit=53,
        micros=10,
    )
    d_tokens = call(
        finish_kernel,
        "finish_plain",
        field,
        values, gradient, d_packed, qkv_weights, unplain,
        fetch={2: None, 3: 0, 0: None, 1: None, 4: None},
        limit=LARGE,
        micros=5,
    )
    sent_one, parts_two = lax.optimization_barrier((sent_one, parts_two))
    chunks_one = core_reduced(kept_one, sent_one)
    d_tokens, grad_qkv, grad_proj = reduced(chunks_one, parts_two, d_tokens)
    return d_tokens.reshape(tokens.shape), grad_qkv, grad_proj


def solution(mesh):
    return jax.shard_map(
        body,
        mesh=mesh,
        in_specs=(P(None, "lat", "lon", None), P(None, "lat", "lon", None), P(), P()),
        out_specs=(P(None, "lat", "lon", None), P(None, "lat", "lon"), P(None, "lat", "lon")),
        check_vma=False,
    )
```
